32 devices in a mesh: ply: 2 (over x), gx: 4 (over y, core), gy: 4 (over z).
Axes of the slice: x: 2, y: 2, z: 4, core: 2. Of those that a mesh axis runs over, the one named last changes fastest.
Arguments:
- coords: float32 [3, 2, 24, 24, 128], P(None, 'ply', 'gx', 'gy'), may hold values from 0 to 1
- strain: float32 [2, 24, 24, 128], P('ply', 'gx', 'gy'), may hold values from 0.1 to 10.1
- kappa_old: float32 [2, 24, 24, 128], P('ply', 'gx', 'gy'), may hold values from 1 to 3
- counts: int32 [2, 24, 24], P('ply', 'gx', 'gy'), may hold values from 0 to 128, as said below
- pair_mask: int32 [2, 24, 24, 26], P('ply', 'gx', 'gy'), may hold values from 0 to 1, as said below
Outputs:
- kappa_new: float32 [2, 24, 24, 128], P('ply', 'gx', 'gy')
- damage: float32 [2, 24, 24, 128], P('ply', 'gx', 'gy')
The draws below stay inside these ranges and needn't reach their ends.
Inputs may be any that keep to these rules, and one draw needn't show every extreme that they name: `counts`: blocks whose count is 0 form the plate's hole, the same through the thickness. pair_mask[a, k] equals pair_mask[a + o_k, 25 - k], o_k being the k-th offset, wherever both blocks lie in the grid.
All inputs are finite; a program needn't handle non-finite values.
Results may differ from the reference program's by a relative error of at most 0.0003.
Values sent between devices are 32-bit elements; how exact they have to be, the bound alone decides.
A program may use at most 64 MiB of HBM per device.

```python
import math
import jax
import jax.numpy as jnp
from jax import lax

PTS = 128
NZ = 2
NX = 24
NY = 24


def make_offsets_drawn():
    listed = []
    for first in (-1, 0, 1):
        for second in (-1, 0, 1):
            for third in (-1, 0, 1):
                if (first, second, third) != (0, 0, 0):
                    listed.append((first, second, third))
    return listed


def draw_coords(key, part):
    side_key, depth_key = jax.random.split(jax.random.fold_in(key, 41))
    toward_high = jax.random.randint(side_key, (3, NZ, NX, NY, 1), 0, 2).astype(jnp.float32)
    spread = jax.random.uniform(depth_key, (3, NZ, NX, NY, PTS), jnp.float32, 0.0, 1.0)
    depth = spread * spread
    placed = toward_high * (1.0 - depth) + (1.0 - toward_high) * depth
    return placed.astype(jnp.float32)


def draw_strain(key, part):
    first_key = jax.random.fold_in(jax.random.fold_in(key, 11), 0)
    third_key = jax.random.fold_in(jax.random.fold_in(key, 11), 2)
    fourth_key = jax.random.fold_in(jax.random.fold_in(key, 11), 3)
    center = jax.random.uniform(third_key, (2,), jnp.float32, -0.9, 0.9)
    across = (2.0 * jnp.arange(NX, dtype=jnp.float32) + 1.0 - NX) / NX
    along = (2.0 * jnp.arange(NY, dtype=jnp.float32) + 1.0 - NY) / NY
    off_x = across[:, None] - center[0]
    off_y = along[None, :] - center[1]
    bump = 1.0 + 2.0 * jnp.exp(-(off_x * off_x + off_y * off_y) / 0.245)
    block_factor = jnp.exp(jax.random.uniform(fourth_key, (NZ, NX, NY, 1), jnp.float32, math.log(0.7), math.log(1.5)))
    base = jnp.exp(jax.random.uniform(first_key, (NZ, NX, NY, PTS), jnp.float32, math.log(0.3), math.log(1.5)))
    return (base * block_factor * bump[None, :, :, None]).astype(jnp.float32)


def draw_counts(key, part):
    across = jnp.arange(NX, dtype=jnp.int32)
    along = jnp.arange(NY, dtype=jnp.int32)
    scaled_x = (2 * across + 1 - NX) * 512 // NX
    scaled_y = (2 * along + 1 - NY) * 512 // NY
    inside = scaled_x[:, None] * scaled_x[:, None] + scaled_y[None, :] * scaled_y[None, :] < 28900
    filled = jax.random.randint(jax.random.fold_in(key, 23), (NZ, NX, NY), 16, 129)
    return jnp.where(inside[None], 0, filled).astype(jnp.int32)


def draw_pair_mask(key, part):
    near_offsets = make_offsets_drawn()
    halves = (jax.random.randint(jax.random.fold_in(key, 37), (NZ, NX, NY, 13), 0, 4) < 3).astype(jnp.int32)
    columns = [None] * 26
    for which in range(13):
        forward = near_offsets[13 + which]
        columns[13 + which] = halves[..., which]
        columns[12 - which] = jnp.roll(halves[..., which], forward, axis=(0, 1, 2))
    return jnp.stack(columns, -1).astype(jnp.int32)


def steps_of(rng, dims, cuts, smallest, largest):
    def one(dim, shards_of):
        draws = jax.random.uniform(jax.random.fold_in(jax.random.fold_in(rng, 6), dim), (shards_of,), jnp.float32, smallest / len(cuts), largest / len(cuts))
        return jnp.repeat(jnp.exp(draws), dims[dim] // shards_of).reshape((-1,) + (1,) * (len(dims) - dim - 1))

    level = one(*cuts[0])
    for cut in cuts[1:]:
        level = level * one(*cut)
    return level


def setup_inputs(seed: int = 0) -> dict:
    key_of = jax.random.split(jax.random.key(seed), 6)
    coords = draw_coords(jax.random.fold_in(key_of[5], 71), 0)
    strain = draw_strain(jax.random.fold_in(key_of[5], 71), 0)
    kappa_old = jnp.clip(jnp.exp(math.log(3.0) - 1.0986123 * jax.random.uniform(key_of[2], (NZ, NX, NY, PTS), jnp.float32) ** steps_of(key_of[2], (NZ, NX, NY, PTS), ((0, 2), (1, 4), (2, 4)), -0.2, 0.2)), 1.0, 3.0)
    counts = draw_counts(jax.random.fold_in(key_of[5], 71), 0)
    pair_mask = draw_pair_mask(jax.random.fold_in(key_of[5], 71), 0)
    return {"coords": coords, "strain": strain, "kappa_old": kappa_old, "counts": counts, "pair_mask": pair_mask}


def make_offsets():
    listed = []
    for first in (-1, 0, 1):
        for second in (-1, 0, 1):
            for third in (-1, 0, 1):
                listed.append((first, second, third))
    return listed


def bell_weights(center, beside, offset):
    squared = jnp.zeros((center.shape[1], center.shape[2], center.shape[2]), jnp.float32)
    for comp in range(3):
        gap = offset[comp] + beside[comp][:, None, :] - center[comp][:, :, None]
        squared = squared + gap * gap
    return jnp.square(jnp.maximum(0.0, 1.0 - squared))


def reference(coords, strain, kappa_old, counts, pair_mask):
    every_offset = make_offsets()
    slots = lax.broadcasted_iota(jnp.int32, strain.shape, 3)
    active = (slots < counts[..., None]).astype(jnp.float32)
    payload = jnp.concatenate([coords, (strain * active)[None], active[None]], 0)
    padded = jnp.pad(payload, ((0, 0), (1, 1), (1, 1), (1, 1), (0, 0)))

    def one_row(row_at):
        zero = row_at * 0
        layer_at = row_at // NX
        strip_at = row_at % NX
        window = lax.dynamic_slice(padded, (zero, layer_at, strip_at, zero, zero), (5, 3, 3, NY + 2, PTS))
        pair_flags = lax.dynamic_slice(pair_mask, (layer_at, strip_at, zero, zero), (1, 1, NY, 26))[0, 0].astype(jnp.float32)
        center = window[:, 1, 1, 1:NY + 1]
        totals = jnp.zeros((2, NY, PTS), jnp.float32)
        for which, offset in enumerate(every_offset):
            beside = window[:, 1 + offset[0], 1 + offset[1], 1 + offset[2]:1 + offset[2] + NY]
            weights = bell_weights(center, beside, offset)
            term = jnp.einsum('bij,cbj->cbi', weights, beside[3:5], precision=lax.Precision.HIGHEST)
            if offset != (0, 0, 0):
                flag_at = which if which < 13 else which - 1
                term = term * pair_flags[:, flag_at][None, :, None]
            totals = totals + term
        return totals

    totals = lax.map(one_row, jnp.arange(NZ * NX, dtype=jnp.int32))
    totals = totals.reshape(NZ, NX, 2, NY, PTS).transpose(2, 0, 1, 3, 4)
    weighted, weight_sum = totals[0], totals[1]
    averaged = active * weighted / (weight_sum + 1.0 - active)
    highest = jnp.max(averaged) + 1e-6
    kappa_new = jnp.maximum(kappa_old, 4.0 * averaged / highest)
    damage = active * (1.0 - jnp.exp(-(kappa_new - 1.0) / 2.5) / kappa_new)
    return kappa_new, damage
```

```python
import functools

import jax
import jax.numpy as jnp
from jax import lax
from jax.experimental import pallas as pl
from jax.experimental.pallas import tpu as pltpu
from jax.sharding import PartitionSpec as P

MESH = pl.DeviceIdType.MESH
AXES = ("ply", "gx", "gy")
FAR = -1e30
ROWS = 32
FULL_VMEM = 48 * 1024 * 1024


def directions():
    listed = []
    for layer in (0, 1):
        for dx in (-1, 0, 1):
            for dy in (-1, 0, 1):
                if (layer, dx, dy) != (0, 0, 0):
                    listed.append((layer, dx, dy))
    return listed


def send_span(step, size):
    return {-1: (1, 1), 0: (1, size), 1: (size, 1)}[step]


def land_span(step, size):
    return {-1: (0, 1), 0: (1, size), 1: (size + 1, 1)}[step]


def halo_kernel(sizes, counts_ref, coords_ref, strain_ref, out_ref, send_sem, recv_sem):
    across, along = strain_ref.shape[1], strain_ref.shape[2]
    ply, gx, gy = (lax.axis_index(axis) for axis in AXES)
    listed = directions()

    def exists(dx, dy):
        x, y = gx + dx, gy + dy
        return (x >= 0) & (x < sizes[1]) & (y >= 0) & (y < sizes[2])

    def peer(layer, dx, dy):
        return (1 - ply if layer else ply, gx + dx, gy + dy)

    barrier = pltpu.get_barrier_semaphore()
    for layer, dx, dy in listed:
        @pl.when(exists(dx, dy))
        def _():
            pl.semaphore_signal(barrier, inc=1, device_id=peer(layer, dx, dy), device_id_type=MESH)

    slots = lax.broadcasted_iota(jnp.int32, (1, strain_ref.shape[3]), 1)
    for x in range(across):
        for y in range(along):
            for comp in range(3):
                out_ref[0, x + 1, y + 1, pl.ds(comp, 1), :] = coords_ref[comp, 0, x, pl.ds(y, 1), :]
            live = slots < counts_ref[0, x, y]
            out_ref[0, x + 1, y + 1, pl.ds(3, 1), :] = jnp.where(live, strain_ref[0, x, pl.ds(y, 1), :], 0.0)

    wide = 1 + (gx > 0).astype(jnp.int32) + (gx < sizes[1] - 1).astype(jnp.int32)
    deep = 1 + (gy > 0).astype(jnp.int32) + (gy < sizes[2] - 1).astype(jnp.int32)
    pl.semaphore_wait(barrier, 2 * wide * deep - 1)

    def sending(which):
        layer, dx, dy = listed[which]
        (x0, nx), (y0, ny) = send_span(dx, across), send_span(dy, along)
        (u0, _), (v0, _) = land_span(-dx, across), land_span(-dy, along)
        return pltpu.make_async_remote_copy(
            src_ref=out_ref.at[0, pl.ds(x0, nx), pl.ds(y0, ny)],
            dst_ref=out_ref.at[layer, pl.ds(u0, nx), pl.ds(v0, ny)],
            send_sem=send_sem.at[which],
            recv_sem=recv_sem.at[which],
            device_id=peer(layer, dx, dy),
            device_id_type=MESH,
        )

    order = sorted(range(len(listed)), key=lambda which: (listed[which][1:] != (0, 0), -listed[which][0]))
    for which in order:
        @pl.when(exists(*listed[which][1:]))
        def _():
            sending(which).start()

    for which in order:
        layer, dx, dy = listed[which]

        @pl.when(exists(dx, dy))
        def _():
            (u0, nx), (v0, ny) = land_span(dx, across), land_span(dy, along)
            (x0, _), (y0, _) = send_span(dx, across), send_span(dy, along)
            arriving = pltpu.make_async_remote_copy(
                src_ref=out_ref.at[0, pl.ds(x0, nx), pl.ds(y0, ny)],
                dst_ref=out_ref.at[layer, pl.ds(u0, nx), pl.ds(v0, ny)],
                send_sem=send_sem.at[which],
                recv_sem=recv_sem.at[listed.index((layer, -dx, -dy))],
                device_id=peer(layer, dx, dy),
                device_id_type=MESH,
            )
            arriving.wait_recv()
            sending(which).wait_send()


def average_kernel(across, along, lists_ref, counts_ref, side_ref, pack_ref, out_ref, source, column, total_w, total_s):
    points = out_ref.shape[3]
    wide, deep = across + 2, along + 2
    listed = lists_ref.shape[0] // (across * along)
    side = side_ref[0].astype(jnp.float32)
    down = lax.broadcasted_iota(jnp.int32, (deep, points), 0).astype(jnp.float32)

    for layer in range(2):
        for x in range(wide):
            at = (layer * wide + x) * deep
            place = (layer * side - 0.5, x - 0.5 * wide, down - 0.5 * deep)
            squared = jnp.zeros((deep, points), jnp.float32)
            for comp in range(3):
                spot = pack_ref[layer, x, :, comp, :] + place[comp]
                source[comp, pl.ds(at, deep), :] = spot
                squared = squared + spot * spot
            strain = pack_ref[layer, x, :, 3, :]
            source[3, pl.ds(at, deep), :] = jnp.where(strain > 0.0, -squared, FAR)
            source[4, pl.ds(at, deep), :] = strain
    for comp in range(5):
        fill = FAR if comp == 3 else 0.0
        source[comp, pl.ds(2 * wide * deep, 8), :] = jnp.full((8, points), fill, jnp.float32)

    for x in range(across):
        for y in range(along):
            at = (x + 1) * deep + y + 1
            spots = [2.0 * source[comp, pl.ds(at, 1), :] for comp in range(3)]
            rows = spots + [1.0 + source[3, pl.ds(at, 1), :], jnp.zeros((4, points), jnp.float32)]
            column[x * along + y] = jnp.concatenate(rows, 0).T

    def one_target(target, carry):
        base = target * listed
        pairs = lists_ref[base + listed - 1]

        def one_group(group, carry):
            at = pl.multiple_of(group * ROWS, ROWS)
            held = column[target, pl.ds(at, ROWS), :]
            spot = [jnp.broadcast_to(held[:, c : c + 1], (ROWS, points)) for c in range(4)]

            def one_pair(pair, sums):
                sum_w, sum_s = sums
                for half in range(2):
                    index = lists_ref[base + 2 * pair + half]
                    row = [source[c, pl.ds(index, 1), :] for c in range(5)]
                    inside = spot[0] * row[0] + spot[1] * row[1] + (spot[2] * row[2] + (spot[3] + row[3]))
                    inside = jnp.maximum(inside, 0.0)
                    weight = inside * inside
                    sum_w = sum_w + weight
                    sum_s = sum_s + weight * row[4]
                return sum_w, sum_s

            zero = jnp.zeros((ROWS, points), jnp.float32)
            sum_w, sum_s = lax.fori_loop(0, pairs, one_pair, (zero, zero))
            total_w[target, pl.ds(at, ROWS), :] = sum_w
            total_s[target, pl.ds(at, ROWS), :] = sum_s
            return carry

        return lax.fori_loop(0, (counts_ref[target] + ROWS - 1) // ROWS, one_group, carry)

    lax.fori_loop(0, across * along, one_target, 0)

    ones = jnp.ones((8, 2 * points), jnp.bfloat16)
    slots = lax.broadcasted_iota(jnp.int32, (1, points), 1)

    def lane_sums(block):
        high = block.astype(jnp.bfloat16)
        low = (block - high.astype(jnp.float32)).astype(jnp.bfloat16)
        both = jnp.concatenate([high, low], axis=1)
        summed = lax.dot_general(ones, both, (((1,), (1,)), ((), ())), preferred_element_type=jnp.float32)
        return summed[0:1]

    def finish(x, carry):
        for y in range(along):
            target = x * along + y
            weight_sum = lane_sums(total_w[target])
            weighted = lane_sums(total_s[target])
            live = slots < counts_ref[target]
            out_ref[0, x, pl.ds(y, 1), :] = jnp.where(live, weighted / jnp.where(live, weight_sum, 1.0), 0.0)
        return carry

    lax.fori_loop(0, across, finish, 0)


def highest_kernel(sizes, averaged_ref, out_ref, held, send_sem, recv_sem):
    ply, gx, gy = (lax.axis_index(axis) for axis in AXES)
    mine = ply * sizes[1] + gx
    first = sizes[0] * sizes[1]
    rounds = (
        [(1 + k, lax.rem(mine + 1 + k, first)) for k in range(first - 1)],
        [(1 + k, lax.rem(gy + 1 + k, sizes[2])) for k in range(sizes[2] - 1)],
    )

    def peer(which, index):
        return (index // sizes[1], lax.rem(index, sizes[1]), gy) if which == 0 else (ply, gx, index)

    barrier = pltpu.get_barrier_semaphore()
    for which in range(2):
        for _, index in rounds[which]:
            pl.semaphore_signal(barrier, inc=1, device_id=peer(which, index), device_id_type=MESH)
    best = jnp.max(averaged_ref[0])
    pl.semaphore_wait(barrier, len(rounds[0]) + len(rounds[1]))

    at = 0
    for which in range(2):
        held[at] = jnp.full(held.shape[1:], best, jnp.float32)
        copies = []
        for step, index in rounds[which]:
            copies.append(
                pltpu.make_async_remote_copy(
                    src_ref=held.at[at],
                    dst_ref=held.at[at + step],
                    send_sem=send_sem.at[at + step],
                    recv_sem=recv_sem.at[at + step],
                    device_id=peer(which, index),
                    device_id_type=MESH,
                )
            )
        for copy in copies:
            copy.start()
        for copy in copies:
            copy.wait()
        best = held[at]
        for step, _ in rounds[which]:
            best = jnp.maximum(best, held[at + step])
        best = best if which else jnp.max(best)
        at += len(rounds[which]) + 1
    out_ref[...] = best


def source_lists(pair_mask, sizes):
    across, along = pair_mask.shape[1:3]
    ply, gx, gy = (lax.axis_index(axis) for axis in AXES)
    wide, deep = across + 2, along + 2
    mask = pair_mask[0]
    other = jnp.where(ply == 0, mask[..., 17:26], mask[..., 0:9])
    itself = jnp.ones_like(mask[..., :1])
    flags = jnp.concatenate([mask[..., 9:13], itself, mask[..., 13:17], other], -1)
    k = jnp.arange(18, dtype=jnp.int32)
    layer, dx, dy = k // 9, k // 3 % 3 - 1, k % 3 - 1
    x = jnp.arange(across, dtype=jnp.int32)[:, None, None]
    y = jnp.arange(along, dtype=jnp.int32)[None, :, None]
    px, py = gx * across + x + dx, gy * along + y + dy
    inside = (px >= 0) & (px < sizes[1] * across) & (py >= 0) & (py < sizes[2] * along)
    taken = (flags > 0) & inside
    index = (layer * wide + x + dx + 1) * deep + y + dy + 1
    spare = 2 * wide * deep
    before = jnp.sum(jnp.where((k[None, :] < k[:, None]) & taken[..., None, :], 1, 0), -1)
    number = jnp.sum(taken.astype(jnp.int32), -1, keepdims=True)
    put = taken[..., None, :] & (before[..., None, :] == k[:, None])
    entries = spare + jnp.sum(jnp.where(put, index[..., None, :] - spare, 0), -1)
    return jnp.concatenate([entries, jnp.full_like(number, spare), (number + 1) // 2], -1).reshape(-1)


def on_device(sizes, coords, strain, kappa_old, counts, pair_mask):
    layers, across, along, points = strain.shape
    assert layers == 1 and sizes[0] == 2
    wide, deep = across + 2, along + 2
    vmem = pl.BlockSpec(memory_space=pltpu.VMEM)
    smem = pl.BlockSpec(memory_space=pltpu.SMEM)
    many = len(directions())
    packed = pl.pallas_call(
        functools.partial(halo_kernel, sizes),
        out_shape=jax.ShapeDtypeStruct((2, wide, deep, 4, points), jnp.float32),
        in_specs=[smem, vmem, vmem],
        out_specs=vmem,
        scratch_shapes=[pltpu.SemaphoreType.DMA((many,)), pltpu.SemaphoreType.DMA((many,))],
        compiler_params=pltpu.CompilerParams(collective_id=0, has_side_effects=True),
    )(counts, coords, strain)

    lists = source_lists(pair_mask, sizes)
    side = (1 - 2 * lax.axis_index("ply")).astype(jnp.int32).reshape(1)
    targets = across * along
    averaged = pl.pallas_call(
        functools.partial(average_kernel, across, along),
        out_shape=jax.ShapeDtypeStruct(strain.shape, jnp.float32),
        in_specs=[smem, smem, smem, vmem],
        out_specs=vmem,
        scratch_shapes=[
            pltpu.VMEM((5, 2 * wide * deep + 8, points), jnp.float32),
            pltpu.VMEM((targets, points, 8), jnp.float32),
            pltpu.VMEM((targets, points, points), jnp.float32),
            pltpu.VMEM((targets, points, points), jnp.float32),
        ],
        compiler_params=pltpu.CompilerParams(vmem_limit_bytes=FULL_VMEM),
    )(lists, counts.reshape(-1), side, packed)

    slots = sizes[0] * sizes[1] + sizes[2]
    highest = pl.pallas_call(
        functools.partial(highest_kernel, sizes),
        out_shape=jax.ShapeDtypeStruct((8, points), jnp.float32),
        in_specs=[vmem],
        out_specs=vmem,
        scratch_shapes=[
            pltpu.VMEM((slots, 8, points), jnp.float32),
            pltpu.SemaphoreType.DMA((slots,)),
            pltpu.SemaphoreType.DMA((slots,)),
        ],
        compiler_params=pltpu.CompilerParams(collective_id=1, has_side_effects=True),
    )(averaged)
    highest = highest[0:1, :] + 1e-06

    live = lax.broadcasted_iota(jnp.int32, strain.shape, 3) < counts[..., None]
    kappa_new = jnp.maximum(kappa_old, 4.0 * averaged / highest)
    damage = jnp.where(live, 1.0 - jnp.exp(-(kappa_new - 1.0) / 2.5) / kappa_new, 0.0)
    return (kappa_new, damage)


def solution(mesh):
    placed = (
        P(None, "ply", "gx", "gy", None),
        P("ply", "gx", "gy", None),
        P("ply", "gx", "gy", None),
        P("ply", "gx", "gy"),
        P("ply", "gx", "gy", None),
    )
    sizes = tuple(mesh.shape[axis] for axis in AXES)
    return jax.shard_map(
        functools.partial(on_device, sizes),
        mesh=mesh,
        in_specs=placed,
        out_specs=(P("ply", "gx", "gy", None), P("ply", "gx", "gy", None)),
        check_vma=False,
    )
```

```python
import functools

import jax
import jax.numpy as jnp
from jax import lax
from jax.experimental import pallas as pl
from jax.experimental.pallas import tpu as pltpu
from jax.sharding import PartitionSpec as P

MESH = pl.DeviceIdType.MESH
AXES = ("ply", "gx", "gy")
FAR = -1e30
ROWS = 32
DEPTH = 32
FULL_VMEM = 48 * 1024 * 1024


def directions():
    listed = []
    for layer in (0, 1):
        for dx in (-1, 0, 1):
            for dy in (-1, 0, 1):
                if (layer, dx, dy) != (0, 0, 0):
                    listed.append((layer, dx, dy))
    return listed


def send_span(step, size):
    return {-1: (1, 1), 0: (1, size), 1: (size, 1)}[step]


def land_span(step, size):
    return {-1: (0, 1), 0: (1, size), 1: (size + 1, 1)}[step]


def damage_kernel(sizes, counts_ref, mask_ref, coords_ref, strain_ref, kappa_ref, kappa_out, damage_out,
                  pack, source, target_side, total_w, total_s, averaged, held, send_sem, recv_sem, max_send, max_recv):
    across, along, points = strain_ref.shape[1:]
    wide, deep = across + 2, along + 2
    ply, gx, gy = (lax.axis_index(axis) for axis in AXES)
    listed = directions()

    def exists(dx, dy):
        x, y = gx + dx, gy + dy
        return (x >= 0) & (x < sizes[1]) & (y >= 0) & (y < sizes[2])

    def peer(layer, dx, dy):
        return (1 - ply if layer else ply, gx + dx, gy + dy)

    mine = ply * sizes[1] + gx
    first = sizes[0] * sizes[1]
    rounds = (
        [(1 + k, lax.rem(mine + 1 + k, first)) for k in range(first - 1)],
        [(1 + k, lax.rem(gy + 1 + k, sizes[2])) for k in range(sizes[2] - 1)],
    )

    def max_peer(which, index):
        return (index // sizes[1], lax.rem(index, sizes[1]), gy) if which == 0 else (ply, gx, index)

    pack[...] = jnp.zeros(pack.shape, jnp.float32)
    barrier = pltpu.get_barrier_semaphore()
    for layer, dx, dy in listed:
        @pl.when(exists(dx, dy))
        def _():
            pl.semaphore_signal(barrier, inc=1, device_id=peer(layer, dx, dy), device_id_type=MESH)
    for which in range(2):
        for _, index in rounds[which]:
            pl.semaphore_signal(barrier, inc=1, device_id=max_peer(which, index), device_id_type=MESH)

    slots = lax.broadcasted_iota(jnp.int32, (1, points), 1)
    for x in range(across):
        for y in range(along):
            for comp in range(3):
                pack[0, x + 1, y + 1, pl.ds(comp, 1), :] = coords_ref[comp, 0, x, pl.ds(y, 1), :]
            live = slots < counts_ref[0, x, y]
            pack[0, x + 1, y + 1, pl.ds(3, 1), :] = jnp.where(live, strain_ref[0, x, pl.ds(y, 1), :], 0.0)

    wide_peers = 1 + (gx > 0).astype(jnp.int32) + (gx < sizes[1] - 1).astype(jnp.int32)
    deep_peers = 1 + (gy > 0).astype(jnp.int32) + (gy < sizes[2] - 1).astype(jnp.int32)
    pl.semaphore_wait(barrier, 2 * wide_peers * deep_peers - 1 + len(rounds[0]) + len(rounds[1]))

    def sending(which):
        layer, dx, dy = listed[which]
        (x0, nx), (y0, ny) = send_span(dx, across), send_span(dy, along)
        (u0, _), (v0, _) = land_span(-dx, across), land_span(-dy, along)
        return pltpu.make_async_remote_copy(
            src_ref=pack.at[0, pl.ds(x0, nx), pl.ds(y0, ny)],
            dst_ref=pack.at[layer, pl.ds(u0, nx), pl.ds(v0, ny)],
            send_sem=send_sem.at[which],
            recv_sem=recv_sem.at[which],
            device_id=peer(layer, dx, dy),
            device_id_type=MESH,
        )

    order = sorted(range(len(listed)), key=lambda which: (listed[which][1:] != (0, 0), -listed[which][0]))
    for which in order:
        @pl.when(exists(*listed[which][1:]))
        def _():
            sending(which).start()

    side = (1 - 2 * ply).astype(jnp.float32)
    sub = lax.broadcasted_iota(jnp.int32, (8, points), 0)
    top = sub < 4
    row = jnp.where(top, sub, sub - 4)
    last = jnp.where(top, 1.0, 0.0)

    def split(rows):
        high = rows.astype(jnp.bfloat16).astype(jnp.float32)
        rest = rows - high
        middle = rest.astype(jnp.bfloat16).astype(jnp.float32)
        return high, middle, rest - middle

    def spots(layer, x, y):
        origin = (layer * side - 0.5, x - 0.5 * wide, y - 0.5 * deep)
        found = [
            jnp.broadcast_to(pack[layer, x, y, pl.ds(comp, 1), :], (8, points)) + origin[comp] for comp in range(3)
        ]
        return found, found[0] * found[0] + found[1] * found[1] + found[2] * found[2]

    def stack(rows):
        return jnp.where(row == 0, rows[0], jnp.where(row == 1, rows[1], jnp.where(row == 2, rows[2], rows[3])))

    def build_source(layer, x, y, found, squared):
        strain = jnp.broadcast_to(pack[layer, x, y, pl.ds(3, 1), :], (8, points))
        high, middle, low = split(stack(found + [jnp.where(strain > 0.0, -squared, FAR)]))
        pair = jnp.where(top, high, middle)
        rows = jnp.concatenate([pair, jnp.where(top, high, low), pair, last], 0)
        source[layer, x, :, pl.ds(y * points, points)] = rows.astype(jnp.bfloat16)

    def build_target(x, y, found, squared):
        high, middle, low = split(stack([2.0 * spot for spot in found] + [jnp.ones((8, points), jnp.float32)]))
        a_high, a_middle, a_low = split(1.0 - squared)
        own = jnp.where(sub == 0, a_high, jnp.where(sub == 1, a_middle, jnp.where(sub == 2, a_low, 0.0)))
        rows = jnp.concatenate([high, jnp.where(top, middle, high), jnp.where(top, low, middle), own], 0)
        target_side[(x - 1) * along + y - 1] = rows.T.astype(jnp.bfloat16)

    def own_row(x, carry):
        for y in range(1, along + 1):
            found, squared = spots(0, x, y)
            build_source(0, x, y, found, squared)
            build_target(x, y, found, squared)
        return carry

    lax.fori_loop(1, across + 1, own_row, 0)

    mask_base = jnp.where(ply == 0, 17, 0)

    def mask_of(layer, x, y, near):
        if layer:
            return mask_ref[0, x, y, mask_base + near].astype(jnp.float32)
        if near == 4:
            return None
        return mask_ref[0, x, y, 9 + near - (near > 4)].astype(jnp.float32)

    def sums_of(x, y, layer):
        beside = jnp.concatenate(
            [source[layer, x + step, :, pl.ds(y * points, 3 * points)] for step in range(3)], axis=1
        )
        inside = jnp.dot(target_side[x * along + y], beside, preferred_element_type=jnp.float32)
        flags, strains = [], []
        for near in range(9):
            strain = pack[layer, x + near // 3, y + near % 3, pl.ds(3, 1), :]
            flag = mask_of(layer, x, y, near)
            flags.append(flag)
            strains.append(strain if flag is None else strain * flag)
        parts = []
        for at in range(0, points, ROWS):
            sum_w = sum_s = None
            for near in range(9):
                weight = jnp.maximum(inside[at : at + ROWS, near * points : (near + 1) * points], 0.0)
                weight = weight * weight
                term_w = weight if flags[near] is None else weight * flags[near]
                term_s = weight * strains[near]
                sum_w = term_w if sum_w is None else sum_w + term_w
                sum_s = term_s if sum_s is None else sum_s + term_s
            parts.append((at, sum_w, sum_s))
        return parts

    def own_layer(x, ys):
        for y in ys:
            for at, sum_w, sum_s in sums_of(x, y, 0):
                total_w[x * along + y, pl.ds(at, ROWS), :] = sum_w
                total_s[x * along + y, pl.ds(at, ROWS), :] = sum_s

    def inner_row(x, carry):
        own_layer(x, range(1, along - 1))
        return carry

    lax.fori_loop(1, across - 1, inner_row, 0)

    for which in order:
        layer, dx, dy = listed[which]

        @pl.when(exists(dx, dy))
        def _():
            (u0, nx), (v0, ny) = land_span(dx, across), land_span(dy, along)
            (x0, _), (y0, _) = send_span(dx, across), send_span(dy, along)
            arriving = pltpu.make_async_remote_copy(
                src_ref=pack.at[0, pl.ds(x0, nx), pl.ds(y0, ny)],
                dst_ref=pack.at[layer, pl.ds(u0, nx), pl.ds(v0, ny)],
                send_sem=send_sem.at[which],
                recv_sem=recv_sem.at[listed.index((layer, -dx, -dy))],
                device_id=peer(layer, dx, dy),
                device_id_type=MESH,
            )
            arriving.wait_recv()
            sending(which).wait_send()

    def halo_row(x, carry):
        for y in range(deep):
            build_source(1, x, y, *spots(1, x, y))
        for y in (0, deep - 1):
            build_source(0, x, y, *spots(0, x, y))
        return carry

    def halo_end(end, carry):
        x = end * (wide - 1)
        for y in range(1, deep - 1):
            build_source(0, x, y, *spots(0, x, y))
        return carry

    lax.fori_loop(0, wide, halo_row, 0)
    lax.fori_loop(0, 2, halo_end, 0)

    def edge_row(x, carry):
        own_layer(x, (0, along - 1))
        return carry

    def end_row(end, carry):
        own_layer(end * (across - 1), range(along))
        return carry

    lax.fori_loop(1, across - 1, edge_row, 0)
    lax.fori_loop(0, 2, end_row, 0)

    ones = jnp.ones((8, 2 * points), jnp.bfloat16)

    def lane_sums(block):
        high = block.astype(jnp.bfloat16)
        low = (block - high.astype(jnp.float32)).astype(jnp.bfloat16)
        both = jnp.concatenate([high, low], axis=1)
        summed = lax.dot_general(ones, both, (((1,), (1,)), ((), ())), preferred_element_type=jnp.float32)
        return summed[0:1]

    def other_layer(x, carry):
        for y in range(along):
            target = x * along + y
            parts = sums_of(x, y, 1)
            weight_sum = lane_sums(jnp.concatenate([w + total_w[target, pl.ds(at, ROWS), :] for at, w, _ in parts], 0))
            weighted = lane_sums(jnp.concatenate([s + total_s[target, pl.ds(at, ROWS), :] for at, _, s in parts], 0))
            live = slots < counts_ref[0, x, y]
            averaged[x, pl.ds(y, 1), :] = jnp.where(live, weighted / jnp.where(live, weight_sum, 1.0), 0.0)
        return carry

    lax.fori_loop(0, across, other_layer, 0)

    best = jnp.max(averaged[...])
    at = 0
    for which in range(2):
        held[at] = jnp.full(held.shape[1:], best, jnp.float32)
        copies = []
        for step, index in rounds[which]:
            copies.append(
                pltpu.make_async_remote_copy(
                    src_ref=held.at[at],
                    dst_ref=held.at[at + step],
                    send_sem=max_send.at[at + step],
                    recv_sem=max_recv.at[at + step],
                    device_id=max_peer(which, index),
                    device_id_type=MESH,
                )
            )
        for copy in copies:
            copy.start()
        for copy in copies:
            copy.wait()
        best = held[at]
        for step, _ in rounds[which]:
            best = jnp.maximum(best, held[at + step])
        best = best if which else jnp.max(best)
        at += len(rounds[which]) + 1

    scale = 4.0 / (best[0:1] + 1e-06)
    for x in range(across):
        kappa = jnp.maximum(kappa_ref[0, x], averaged[x] * scale)
        kappa_out[0, x] = kappa
        grown = 1.0 - jnp.exp(-(kappa - 1.0) / 2.5) / kappa
        for y in range(along):
            live = slots < counts_ref[0, x, y]
            damage_out[0, x, pl.ds(y, 1), :] = jnp.where(live, grown[y : y + 1], 0.0)


def on_device(sizes, coords, strain, kappa_old, counts, pair_mask):
    layers, across, along, points = strain.shape
    assert layers == 1 and sizes[0] == 2
    wide, deep = across + 2, along + 2
    vmem = pl.BlockSpec(memory_space=pltpu.VMEM)
    smem = pl.BlockSpec(memory_space=pltpu.SMEM)
    many = len(directions())
    targets = across * along
    slots = sizes[0] * sizes[1] + sizes[2]
    return pl.pallas_call(
        functools.partial(damage_kernel, sizes),
        out_shape=(jax.ShapeDtypeStruct(strain.shape, jnp.float32), jax.ShapeDtypeStruct(strain.shape, jnp.float32)),
        in_specs=[smem, smem, vmem, vmem, vmem],
        out_specs=(vmem, vmem),
        scratch_shapes=[
            pltpu.VMEM((2, wide, deep, 4, points), jnp.float32),
            pltpu.VMEM((2, wide, DEPTH, deep * points), jnp.bfloat16),
            pltpu.VMEM((targets, points, DEPTH), jnp.bfloat16),
            pltpu.VMEM((targets, points, points), jnp.float32),
            pltpu.VMEM((targets, points, points), jnp.float32),
            pltpu.VMEM((across, along, points), jnp.float32),
            pltpu.VMEM((slots, 8, points), jnp.float32),
            pltpu.SemaphoreType.DMA((many,)),
            pltpu.SemaphoreType.DMA((many,)),
            pltpu.SemaphoreType.DMA((slots,)),
            pltpu.SemaphoreType.DMA((slots,)),
        ],
        compiler_params=pltpu.CompilerParams(collective_id=0, has_side_effects=True, vmem_limit_bytes=FULL_VMEM),
    )(counts, pair_mask, coords, strain, kappa_old)


def solution(mesh):
    placed = (
        P(None, "ply", "gx", "gy", None),
        P("ply", "gx", "gy", None),
        P("ply", "gx", "gy", None),
        P("ply", "gx", "gy"),
        P("ply", "gx", "gy", None),
    )
    sizes = tuple(mesh.shape[axis] for axis in AXES)
    return jax.shard_map(
        functools.partial(on_device, sizes),
        mesh=mesh,
        in_specs=placed,
        out_specs=(P("ply", "gx", "gy", None), P("ply", "gx", "gy", None)),
        check_vma=False,
    )
```

```python
import functools

import jax
import jax.numpy as jnp
from jax import lax
from jax.experimental import pallas as pl
from jax.experimental.pallas import tpu as pltpu
from jax.sharding import PartitionSpec as P

MESH = pl.DeviceIdType.MESH
AXES = ("ply", "gx", "gy")
FAR = -1e30
ROWS = 64
DEPTH = 32
AHEAD = 2
FULL_VMEM = 48 * 1024 * 1024


def directions():
    listed = []
    for layer in (0, 1):
        for dx in (-1, 0, 1):
            for dy in (-1, 0, 1):
                if (layer, dx, dy) != (0, 0, 0):
                    listed.append((layer, dx, dy))
    return listed


def send_span(step, size):
    return {-1: (1, 1), 0: (1, size), 1: (size, 1)}[step]


def land_span(step, size):
    return {-1: (0, 1), 0: (1, size), 1: (size + 1, 1)}[step]


def damage_kernel(sizes, counts_ref, mask_ref, coords_ref, strain_ref, kappa_ref, kappa_out, damage_out,
                  pack, source, target_side, total_w, total_s, averaged, held, send_sem, recv_sem, max_send, max_recv):
    across, along, _, points = strain_ref.shape
    wide, deep = across + 2, along + 2
    ply, gx, gy = (lax.axis_index(axis) for axis in AXES)
    listed = directions()

    def exists(dx, dy):
        x, y = gx + dx, gy + dy
        return (x >= 0) & (x < sizes[1]) & (y >= 0) & (y < sizes[2])

    def peer(layer, dx, dy):
        return (1 - ply if layer else ply, gx + dx, gy + dy)

    mine = ply * sizes[1] + gx
    first = sizes[0] * sizes[1]
    rounds = (
        [(1 + k, lax.rem(mine + 1 + k, first)) for k in range(first - 1)],
        [(1 + k, lax.rem(gy + 1 + k, sizes[2])) for k in range(sizes[2] - 1)],
    )

    def max_peer(which, index):
        return (index // sizes[1], lax.rem(index, sizes[1]), gy) if which == 0 else (ply, gx, index)

    pack[...] = jnp.zeros(pack.shape, jnp.float32)
    barrier = pltpu.get_barrier_semaphore()
    for layer, dx, dy in listed:
        @pl.when(exists(dx, dy))
        def _():
            pl.semaphore_signal(barrier, inc=1, device_id=peer(layer, dx, dy), device_id_type=MESH)
    for which in range(2):
        for _, index in rounds[which]:
            pl.semaphore_signal(barrier, inc=1, device_id=max_peer(which, index), device_id_type=MESH)

    slots = lax.broadcasted_iota(jnp.int32, (1, points), 1)
    for x in range(across):
        for y in range(along):
            for comp in range(3):
                pack[0, x + 1, y + 1, pl.ds(comp, 1), :] = coords_ref[comp, x, y]
            live = slots < counts_ref[x, 0, y]
            pack[0, x + 1, y + 1, pl.ds(3, 1), :] = jnp.where(live, strain_ref[x, y], 0.0)

    wide_peers = 1 + (gx > 0).astype(jnp.int32) + (gx < sizes[1] - 1).astype(jnp.int32)
    deep_peers = 1 + (gy > 0).astype(jnp.int32) + (gy < sizes[2] - 1).astype(jnp.int32)
    pl.semaphore_wait(barrier, 2 * wide_peers * deep_peers - 1 + len(rounds[0]) + len(rounds[1]))

    def sending(which):
        layer, dx, dy = listed[which]
        (x0, nx), (y0, ny) = send_span(dx, across), send_span(dy, along)
        (u0, _), (v0, _) = land_span(-dx, across), land_span(-dy, along)
        return pltpu.make_async_remote_copy(
            src_ref=pack.at[0, pl.ds(x0, nx), pl.ds(y0, ny)],
            dst_ref=pack.at[layer, pl.ds(u0, nx), pl.ds(v0, ny)],
            send_sem=send_sem.at[which],
            recv_sem=recv_sem.at[which],
            device_id=peer(layer, dx, dy),
            device_id_type=MESH,
        )

    order = sorted(range(len(listed)), key=lambda which: (listed[which][1:] != (0, 0), -listed[which][0]))
    for which in order:
        @pl.when(exists(*listed[which][1:]))
        def _():
            sending(which).start()

    side = (1 - 2 * ply).astype(jnp.float32)
    sub = lax.broadcasted_iota(jnp.int32, (8, points), 0)
    top = sub < 4
    row = jnp.where(top, sub, sub - 4)
    last = jnp.where(top, 1.0, 0.0)

    def split(rows):
        high = rows.astype(jnp.bfloat16).astype(jnp.float32)
        rest = rows - high
        middle = rest.astype(jnp.bfloat16).astype(jnp.float32)
        return high, middle, rest - middle

    def spots(layer, x, y):
        origin = (layer * side - 0.5, x - 0.5 * wide, y - 0.5 * deep)
        found = [
            jnp.broadcast_to(pack[layer, x, y, pl.ds(comp, 1), :], (8, points)) + origin[comp] for comp in range(3)
        ]
        return found, found[0] * found[0] + found[1] * found[1] + found[2] * found[2]

    def stack(rows):
        return jnp.where(row == 0, rows[0], jnp.where(row == 1, rows[1], jnp.where(row == 2, rows[2], rows[3])))

    def build_source(layer, x, y, found, squared):
        strain = jnp.broadcast_to(pack[layer, x, y, pl.ds(3, 1), :], (8, points))
        high, middle, low = split(stack(found + [jnp.where(strain > 0.0, -squared, FAR)]))
        pair = jnp.where(top, high, middle)
        rows = jnp.concatenate([pair, jnp.where(top, high, low), pair, last], 0)
        source[layer, x, :, pl.ds(y * points, points)] = rows.astype(jnp.bfloat16)

    def build_target(x, y, found, squared):
        high, middle, low = split(stack([2.0 * spot for spot in found] + [jnp.ones((8, points), jnp.float32)]))
        a_high, a_middle, a_low = split(1.0 - squared)
        own = jnp.where(sub == 0, a_high, jnp.where(sub == 1, a_middle, jnp.where(sub == 2, a_low, jnp.where(sub == 4, 1.0, 0.0))))
        rows = jnp.concatenate([high, jnp.where(top, middle, high), jnp.where(top, low, middle), own], 0)
        target_side[(x - 1) * along + y - 1] = rows.T.astype(jnp.bfloat16)

    def own_row(x, carry):
        for y in range(1, along + 1):
            found, squared = spots(0, x, y)
            build_source(0, x, y, found, squared)
            build_target(x, y, found, squared)
        return carry

    lax.fori_loop(1, across + 1, own_row, 0)

    mask_base = jnp.where(ply == 0, 17, 0)

    half_rows = lax.broadcasted_iota(jnp.int32, (DEPTH // 2, points), 0)
    mask_row = jnp.where(half_rows == 12, 1.0, 0.0).astype(jnp.bfloat16)

    def masked_source(layer, x, y, near):
        block = source[layer, x + near // 3, :, pl.ds((y + near % 3) * points, points)]
        if layer == 0 and near == 4:
            return block
        flag = mask_ref[x, y, 0, mask_base + near if layer else 9 + near - (near > 4)]
        away = jnp.full(mask_row.shape, FAR * (1 - flag).astype(jnp.float32)).astype(jnp.bfloat16)
        return jnp.concatenate([block[: DEPTH // 2], block[DEPTH // 2 :] + mask_row * away], 0)

    def row_sums(x, ys, layer):
        tasks = [(y, at, pair) for y in ys for at in range(0, points, ROWS) for pair in range(0, 9, 2)]
        sides = {}

        def product(task):
            y, at, pair = task
            nears = [near for near in (pair, pair + 1) if near < 9]
            for near in nears:
                if (y, near) not in sides:
                    sides[y, near] = masked_source(layer, x, y, near)
            beside = jnp.concatenate([sides[y, near] for near in nears], axis=1)
            rows = target_side[x * along + y, pl.ds(at, ROWS), :]
            return nears, jnp.dot(rows, beside, preferred_element_type=jnp.float32)

        ready = [product(task) for task in tasks[:AHEAD]]
        sum_w = sum_s = None
        for k, (y, at, pair) in enumerate(tasks):
            if k + AHEAD < len(tasks):
                ready.append(product(tasks[k + AHEAD]))
            nears, inside = ready.pop(0)
            for slot, near in enumerate(nears):
                weight = jnp.maximum(inside[:, slot * points : (slot + 1) * points], 0.0)
                weight = weight * weight
                term = weight * pack[layer, x + near // 3, y + near % 3, pl.ds(3, 1), :]
                sum_w = weight if near == 0 else sum_w + weight
                sum_s = term if near == 0 else sum_s + term
            if pair == 8:
                place = (x * along + y, pl.ds(at, ROWS))
                if layer:
                    sum_w = sum_w + total_w[place]
                    sum_s = sum_s + total_s[place]
                total_w[place] = sum_w
                total_s[place] = sum_s

    def own_layer(x, ys):
        row_sums(x, ys, 0)

    def inner_row(x, carry):
        own_layer(x, range(1, along - 1))
        return carry

    lax.fori_loop(1, across - 1, inner_row, 0)

    for which in order:
        layer, dx, dy = listed[which]

        @pl.when(exists(dx, dy))
        def _():
            (u0, nx), (v0, ny) = land_span(dx, across), land_span(dy, along)
            (x0, _), (y0, _) = send_span(dx, across), send_span(dy, along)
            arriving = pltpu.make_async_remote_copy(
                src_ref=pack.at[0, pl.ds(x0, nx), pl.ds(y0, ny)],
                dst_ref=pack.at[layer, pl.ds(u0, nx), pl.ds(v0, ny)],
                send_sem=send_sem.at[which],
                recv_sem=recv_sem.at[listed.index((layer, -dx, -dy))],
                device_id=peer(layer, dx, dy),
                device_id_type=MESH,
            )
            arriving.wait_recv()
            sending(which).wait_send()

    def halo_row(x, carry):
        for y in range(deep):
            build_source(1, x, y, *spots(1, x, y))
        for y in (0, deep - 1):
            build_source(0, x, y, *spots(0, x, y))
        return carry

    def halo_end(end, carry):
        x = end * (wide - 1)
        for y in range(1, deep - 1):
            build_source(0, x, y, *spots(0, x, y))
        return carry

    lax.fori_loop(0, wide, halo_row, 0)
    lax.fori_loop(0, 2, halo_end, 0)

    def edge_row(x, carry):
        own_layer(x, (0, along - 1))
        return carry

    def end_row(end, carry):
        own_layer(end * (across - 1), range(along))
        return carry

    lax.fori_loop(1, across - 1, edge_row, 0)
    lax.fori_loop(0, 2, end_row, 0)

    def other_layer(x, carry):
        row_sums(x, range(along), 1)
        return carry

    lax.fori_loop(0, across, other_layer, 0)

    ones = jnp.ones((8, 2 * points), jnp.bfloat16)

    def lane_sums(block):
        high = block.astype(jnp.bfloat16)
        low = (block - high.astype(jnp.float32)).astype(jnp.bfloat16)
        both = jnp.concatenate([high, low], axis=1)
        summed = lax.dot_general(ones, both, (((1,), (1,)), ((), ())), preferred_element_type=jnp.float32)
        return summed[0:1]

    def divide(x, carry):
        these = pl.ds(x * along, along)
        weight_sum = lane_sums(total_w[these].reshape(along * points, points))
        weighted = lane_sums(total_s[these].reshape(along * points, points))
        for y in range(along):
            span = slice(y * points, (y + 1) * points)
            live = slots < counts_ref[x, 0, y]
            share = weighted[:, span] / jnp.where(live, weight_sum[:, span], 1.0)
            averaged[x, pl.ds(y, 1), :] = jnp.where(live, share, 0.0)
        return carry

    lax.fori_loop(0, across, divide, 0)

    best = jnp.max(averaged[...])
    at = 0
    for which in range(2):
        held[at] = jnp.full(held.shape[1:], best, jnp.float32)
        copies = []
        for step, index in rounds[which]:
            copies.append(
                pltpu.make_async_remote_copy(
                    src_ref=held.at[at],
                    dst_ref=held.at[at + step],
                    send_sem=max_send.at[at + step],
                    recv_sem=max_recv.at[at + step],
                    device_id=max_peer(which, index),
                    device_id_type=MESH,
                )
            )
        for copy in copies:
            copy.start()
        for copy in copies:
            copy.wait()
        best = held[at]
        for step, _ in rounds[which]:
            best = jnp.maximum(best, held[at + step])
        best = best if which else jnp.max(best)
        at += len(rounds[which]) + 1

    scale = 4.0 / (best[0:1] + 1e-06)
    for x in range(across):
        for y in range(along):
            kappa = jnp.maximum(kappa_ref[x, y], averaged[x, pl.ds(y, 1), :] * scale)
            kappa_out[x, y] = kappa
            live = slots < counts_ref[x, 0, y]
            damage_out[x, y] = jnp.where(live, 1.0 - jnp.exp(-(kappa - 1.0) / 2.5) / kappa, 0.0)


def on_device(sizes, coords, strain, kappa_old, counts, pair_mask):
    layers, across, along, points = strain.shape
    assert layers == 1 and sizes[0] == 2
    wide, deep = across + 2, along + 2
    vmem = pl.BlockSpec(memory_space=pltpu.VMEM)
    smem = pl.BlockSpec(memory_space=pltpu.SMEM)
    many = len(directions())
    targets = across * along
    slots = sizes[0] * sizes[1] + sizes[2]
    rows = jax.ShapeDtypeStruct((across, along, 1, points), jnp.float32)
    kappa_new, damage = pl.pallas_call(
        functools.partial(damage_kernel, sizes),
        out_shape=(rows, rows),
        in_specs=[smem, smem, vmem, vmem, vmem],
        out_specs=(vmem, vmem),
        scratch_shapes=[
            pltpu.VMEM((2, wide, deep, 4, points), jnp.float32),
            pltpu.VMEM((2, wide, DEPTH, deep * points), jnp.bfloat16),
            pltpu.VMEM((targets, points, DEPTH), jnp.bfloat16),
            pltpu.VMEM((targets, points, points), jnp.float32),
            pltpu.VMEM((targets, points, points), jnp.float32),
            pltpu.VMEM((across, along, points), jnp.float32),
            pltpu.VMEM((slots, 8, points), jnp.float32),
            pltpu.SemaphoreType.DMA((many,)),
            pltpu.SemaphoreType.DMA((many,)),
            pltpu.SemaphoreType.DMA((slots,)),
            pltpu.SemaphoreType.DMA((slots,)),
        ],
        compiler_params=pltpu.CompilerParams(collective_id=0, has_side_effects=True, vmem_limit_bytes=FULL_VMEM),
    )(
        counts.transpose(1, 0, 2),
        pair_mask.transpose(1, 2, 0, 3),
        coords.transpose(0, 2, 3, 1, 4),
        strain.transpose(1, 2, 0, 3),
        kappa_old.transpose(1, 2, 0, 3),
    )
    return kappa_new.transpose(2, 0, 1, 3), damage.transpose(2, 0, 1, 3)


def solution(mesh):
    placed = (
        P(None, "ply", "gx", "gy", None),
        P("ply", "gx", "gy", None),
        P("ply", "gx", "gy", None),
        P("ply", "gx", "gy"),
        P("ply", "gx", "gy", None),
    )
    sizes = tuple(mesh.shape[axis] for axis in AXES)
    return jax.shard_map(
        functools.partial(on_device, sizes),
        mesh=mesh,
        in_specs=placed,
        out_specs=(P("ply", "gx", "gy", None), P("ply", "gx", "gy", None)),
        check_vma=False,
    )
```

```python
import functools

import jax
import jax.numpy as jnp
from jax import lax
from jax.experimental import pallas as pl
from jax.experimental.pallas import tpu as pltpu
from jax.sharding import PartitionSpec as P

MESH = pl.DeviceIdType.MESH
AXES = ("ply", "gx", "gy")
FAR = -1e30
DEPTH = 48
AHEAD = 1
FULL_VMEM = 58 * 1024 * 1024


def directions():
    listed = []
    for layer in (0, 1):
        for dx in (-1, 0, 1):
            for dy in (-1, 0, 1):
                if (layer, dx, dy) != (0, 0, 0):
                    listed.append((layer, dx, dy))
    return listed


def send_span(step, size):
    return {-1: (1, 1), 0: (1, size), 1: (size, 1)}[step]


def land_span(step, size):
    return {-1: (0, 1), 0: (1, size), 1: (size + 1, 1)}[step]


def damage_kernel(sizes, counts_in, mask_in, coords_in, strain_in, kappa_in, kappa_out, damage_out,
                  counts_ref, mask_ref, coords_ref, strain_ref, kappa_ref, pack, source, shade, target_side,
                  total_w, total_s, averaged, held, in_sem, send_sem, recv_sem, max_send, max_recv):
    across, along, _, points = strain_ref.shape
    wide, deep = across + 2, along + 2
    staged = [
        pltpu.make_async_copy(given, kept, in_sem.at[k])
        for k, (given, kept) in enumerate(
            [(counts_in, counts_ref), (coords_in, coords_ref), (strain_in, strain_ref), (mask_in, mask_ref),
             (kappa_in, kappa_ref)]
        )
    ]
    for copy in staged:
        copy.start()
    ply, gx, gy = (lax.axis_index(axis) for axis in AXES)
    listed = directions()

    def exists(dx, dy):
        x, y = gx + dx, gy + dy
        return (x >= 0) & (x < sizes[1]) & (y >= 0) & (y < sizes[2])

    def peer(layer, dx, dy):
        return (1 - ply if layer else ply, gx + dx, gy + dy)

    mine = ply * sizes[1] + gx
    first = sizes[0] * sizes[1]
    rounds = (
        [(1 + k, lax.rem(mine + 1 + k, first)) for k in range(first - 1)],
        [(1 + k, lax.rem(gy + 1 + k, sizes[2])) for k in range(sizes[2] - 1)],
    )

    def max_peer(which, index):
        return (index // sizes[1], lax.rem(index, sizes[1]), gy) if which == 0 else (ply, gx, index)

    pack[...] = jnp.zeros(pack.shape, jnp.float32)
    barrier = pltpu.get_barrier_semaphore()
    for layer, dx, dy in listed:
        @pl.when(exists(dx, dy))
        def _():
            pl.semaphore_signal(barrier, inc=1, device_id=peer(layer, dx, dy), device_id_type=MESH)
    for which in range(2):
        for _, index in rounds[which]:
            pl.semaphore_signal(barrier, inc=1, device_id=max_peer(which, index), device_id_type=MESH)

    slots = lax.broadcasted_iota(jnp.int32, (1, points), 1)
    for copy in staged[:3]:
        copy.wait()
    for x in range(across):
        for y in range(along):
            for comp in range(3):
                pack[0, x + 1, y + 1, pl.ds(comp, 1), :] = coords_ref[comp, x, y]
            live = slots < counts_ref[x, 0, y]
            pack[0, x + 1, y + 1, pl.ds(3, 1), :] = jnp.where(live, strain_ref[x, y], 0.0)

    wide_peers = 1 + (gx > 0).astype(jnp.int32) + (gx < sizes[1] - 1).astype(jnp.int32)
    deep_peers = 1 + (gy > 0).astype(jnp.int32) + (gy < sizes[2] - 1).astype(jnp.int32)
    pl.semaphore_wait(barrier, 2 * wide_peers * deep_peers - 1 + len(rounds[0]) + len(rounds[1]))

    def sending(which):
        layer, dx, dy = listed[which]
        (x0, nx), (y0, ny) = send_span(dx, across), send_span(dy, along)
        (u0, _), (v0, _) = land_span(-dx, across), land_span(-dy, along)
        return pltpu.make_async_remote_copy(
            src_ref=pack.at[0, pl.ds(x0, nx), pl.ds(y0, ny)],
            dst_ref=pack.at[layer, pl.ds(u0, nx), pl.ds(v0, ny)],
            send_sem=send_sem.at[which],
            recv_sem=recv_sem.at[which],
            device_id=peer(layer, dx, dy),
            device_id_type=MESH,
        )

    order = sorted(range(len(listed)), key=lambda which: (listed[which][1:] != (0, 0), -listed[which][0]))
    for which in order:
        @pl.when(exists(*listed[which][1:]))
        def _():
            sending(which).start()

    side = (1 - 2 * ply).astype(jnp.float32)
    sub = lax.broadcasted_iota(jnp.int32, (8, points), 0)
    top = sub < 4
    row = jnp.where(top, sub, sub - 4)

    def split(rows):
        high = rows.astype(jnp.bfloat16).astype(jnp.float32)
        rest = rows - high
        middle = rest.astype(jnp.bfloat16).astype(jnp.float32)
        return high, middle, rest - middle

    def spots(layer, x, y):
        origin = (layer * side - 0.5, x - 0.5 * wide, y - 0.5 * deep)
        found = [
            jnp.broadcast_to(pack[layer, x, y, pl.ds(comp, 1), :], (8, points)) + origin[comp] for comp in range(3)
        ]
        return found, found[0] * found[0] + found[1] * found[1] + found[2] * found[2]

    def stack(rows):
        return jnp.where(row == 0, rows[0], jnp.where(row == 1, rows[1], jnp.where(row == 2, rows[2], rows[3])))

    def kind(x, y):
        return lax.rem(x, 3) * 3 + y % 3

    def build_source(layer, x, y, found, squared):
        strain = jnp.broadcast_to(pack[layer, x, y, pl.ds(3, 1), :], (8, points))
        high, middle, low = split(stack(found + [jnp.where(strain > 0.0, -squared, FAR)]))
        pair = jnp.where(top, high, middle)
        fourth = jnp.where((sub < 3) | (sub - 4 == kind(x, y)), 1.0, 0.0)
        fifth = jnp.where(sub + 4 == kind(x, y), 1.0, 0.0)
        rows = jnp.concatenate([pair, jnp.where(top, high, low), pair, fourth, fifth, strain], 0).T
        span = pl.ds(y * points, points)
        source[layer, x, span, :] = rows.astype(jnp.bfloat16)
        shade[layer, x, span, :] = jnp.broadcast_to(rows[:, DEPTH - 1 : DEPTH], (points, points))

    mask_base = jnp.where(ply == 0, 17, 0)

    def build_target(x, y, found, squared):
        high, middle, low = split(stack([2.0 * spot for spot in found] + [jnp.ones((8, points), jnp.float32)]))
        a_high, a_middle, a_low = split(1.0 - squared)
        own = jnp.where(sub == 0, a_high, jnp.where(sub == 1, a_middle, jnp.where(sub == 2, a_low, 0.0)))
        fixed = [high, jnp.where(top, middle, high), jnp.where(top, low, middle)]
        zero = jnp.zeros((8, points), jnp.float32)
        for layer in range(2):
            fourth, fifth = own, zero
            for which in range(9):
                near = lax.rem(which // 3 - x + 1 + 3 * wide, 3) * 3 + (which % 3 - y + 1) % 3
                if layer:
                    flag = mask_ref[x - 1, y - 1, 0, mask_base + near]
                else:
                    flag = mask_ref[x - 1, y - 1, 0, 9 + near - (near > 4).astype(jnp.int32)]
                    flag = jnp.where(near == 4, 1, flag)
                away = FAR * (1 - flag).astype(jnp.float32)
                if which < 4:
                    fourth = jnp.where(sub == which + 4, away, fourth)
                else:
                    fifth = jnp.where(sub == which - 4, away, fifth)
            rows = jnp.concatenate(fixed + [fourth, fifth, zero], 0)
            target_side[layer, x - 1, :, pl.ds((y - 1) * points, points)] = rows.astype(jnp.bfloat16)

    staged[3].wait()

    def own_row(x, carry):
        for y in range(1, along + 1):
            found, squared = spots(0, x, y)
            build_source(0, x, y, found, squared)
            build_target(x, y, found, squared)
        return carry

    lax.fori_loop(1, across + 1, own_row, 0)

    def fold(block):
        return jnp.sum(block.reshape(points // 8, 8, points), axis=0)

    def row_sums(x, groups, layer):
        tasks = [(group, step) for group in groups for step in range(3)]

        def product(task):
            (y, many), step = task
            beside = source[layer, x + step, pl.ds(y * points, (many + 2) * points), :]
            these = target_side[layer, x, :, pl.ds(y * points, many * points)]
            return jnp.dot(beside, these, preferred_element_type=jnp.float32)

        ready = [product(task) for task in tasks[:AHEAD]]
        sums = {}
        for k, ((y, many), step) in enumerate(tasks):
            if k + AHEAD < len(tasks):
                ready.append(product(tasks[k + AHEAD]))
            inside = ready.pop(0)
            for block in range(many + 2):
                tint = shade[layer, x + step, pl.ds((y + block) * points, points), :]
                for one in range(many):
                    if not 0 <= block - one <= 2:
                        continue
                    weight = inside[block * points : (block + 1) * points, one * points : (one + 1) * points]
                    weight = jnp.maximum(weight, 0.0)
                    weight = weight * weight
                    sum_w, sum_s = sums.get((y, one), (0.0, 0.0))
                    sums[y, one] = (sum_w + fold(weight), sum_s + fold(weight * tint))
            if step == 2:
                for one in range(many):
                    sum_w, sum_s = sums[y, one]
                    target = x * along + y + one
                    if layer:
                        sum_w = sum_w + total_w[target]
                        sum_s = sum_s + total_s[target]
                    total_w[target] = sum_w
                    total_s[target] = sum_s

    def pairs(start, stop):
        return [(y, min(2, stop - y)) for y in range(start, stop, 2)]

    def inner_row(x, carry):
        row_sums(x, pairs(1, along - 1), 0)
        return carry

    lax.fori_loop(1, across - 1, inner_row, 0)

    for which in order:
        layer, dx, dy = listed[which]

        @pl.when(exists(dx, dy))
        def _():
            (u0, nx), (v0, ny) = land_span(dx, across), land_span(dy, along)
            (x0, _), (y0, _) = send_span(dx, across), send_span(dy, along)
            arriving = pltpu.make_async_remote_copy(
                src_ref=pack.at[0, pl.ds(x0, nx), pl.ds(y0, ny)],
                dst_ref=pack.at[layer, pl.ds(u0, nx), pl.ds(v0, ny)],
                send_sem=send_sem.at[which],
                recv_sem=recv_sem.at[listed.index((layer, -dx, -dy))],
                device_id=peer(layer, dx, dy),
                device_id_type=MESH,
            )
            arriving.wait_recv()
            sending(which).wait_send()

    def halo_row(x, carry):
        for y in range(deep):
            build_source(1, x, y, *spots(1, x, y))
        for y in (0, deep - 1):
            build_source(0, x, y, *spots(0, x, y))
        return carry

    def halo_end(end, carry):
        x = end * (wide - 1)
        for y in range(1, deep - 1):
            build_source(0, x, y, *spots(0, x, y))
        return carry

    lax.fori_loop(0, wide, halo_row, 0)
    lax.fori_loop(0, 2, halo_end, 0)

    def edge_row(x, carry):
        row_sums(x, [(0, 1), (along - 1, 1)], 0)
        return carry

    def end_row(end, carry):
        row_sums(end * (across - 1), pairs(0, along), 0)
        return carry

    def other_layer(x, carry):
        row_sums(x, pairs(0, along), 1)
        return carry

    lax.fori_loop(1, across - 1, edge_row, 0)
    lax.fori_loop(0, 2, end_row, 0)
    lax.fori_loop(0, across, other_layer, 0)

    for x in range(across):
        for y in range(along):
            weight_sum = jnp.sum(total_w[x * along + y], axis=0, keepdims=True)
            weighted = jnp.sum(total_s[x * along + y], axis=0, keepdims=True)
            live = slots < counts_ref[x, 0, y]
            share = weighted / jnp.where(live, weight_sum, 1.0)
            averaged[x, pl.ds(y, 1), :] = jnp.where(live, share, 0.0)

    best = jnp.max(averaged[...])
    at = 0
    for which in range(2):
        held[at] = jnp.full(held.shape[1:], best, jnp.float32)
        copies = []
        for step, index in rounds[which]:
            copies.append(
                pltpu.make_async_remote_copy(
                    src_ref=held.at[at],
                    dst_ref=held.at[at + step],
                    send_sem=max_send.at[at + step],
                    recv_sem=max_recv.at[at + step],
                    device_id=max_peer(which, index),
                    device_id_type=MESH,
                )
            )
        for copy in copies:
            copy.start()
        for copy in copies:
            copy.wait()
        best = held[at]
        for step, _ in rounds[which]:
            best = jnp.maximum(best, held[at + step])
        best = best if which else jnp.max(best)
        at += len(rounds[which]) + 1

    staged[4].wait()
    scale = 4.0 / (best[0:1] + 1e-06)
    for x in range(across):
        for y in range(along):
            kappa = jnp.maximum(kappa_ref[x, y], averaged[x, pl.ds(y, 1), :] * scale)
            kappa_out[x, y] = kappa
            live = slots < counts_ref[x, 0, y]
            damage_out[x, y] = jnp.where(live, 1.0 - jnp.exp(-(kappa - 1.0) / 2.5) / kappa, 0.0)


def on_device(sizes, coords, strain, kappa_old, counts, pair_mask):
    layers, across, along, points = strain.shape
    assert layers == 1 and sizes[0] == 2
    wide, deep = across + 2, along + 2
    vmem = pl.BlockSpec(memory_space=pltpu.VMEM)
    many = len(directions())
    targets = across * along
    slots = sizes[0] * sizes[1] + sizes[2]
    rows = jax.ShapeDtypeStruct((across, along, 1, points), jnp.float32)
    kappa_new, damage = pl.pallas_call(
        functools.partial(damage_kernel, sizes),
        out_shape=(rows, rows),
        in_specs=[pl.BlockSpec(memory_space=pl.ANY)] * 5,
        out_specs=(vmem, vmem),
        scratch_shapes=[
            pltpu.SMEM((across, 1, along), jnp.int32),
            pltpu.SMEM((across, along, 1, pair_mask.shape[3]), jnp.int32),
            pltpu.VMEM((3, across, along, 1, points), jnp.float32),
            pltpu.VMEM((across, along, 1, points), jnp.float32),
            pltpu.VMEM((across, along, 1, points), jnp.float32),
            pltpu.VMEM((2, wide, deep, 4, points), jnp.float32),
            pltpu.VMEM((2, wide, deep * points, DEPTH), jnp.bfloat16),
            pltpu.VMEM((2, wide, deep * points, points), jnp.float32),
            pltpu.VMEM((2, across, DEPTH, along * points), jnp.bfloat16),
            pltpu.VMEM((targets, 8, points), jnp.float32),
            pltpu.VMEM((targets, 8, points), jnp.float32),
            pltpu.VMEM((across, along, points), jnp.float32),
            pltpu.VMEM((slots, 8, points), jnp.float32),
            pltpu.SemaphoreType.DMA((5,)),
            pltpu.SemaphoreType.DMA((many,)),
            pltpu.SemaphoreType.DMA((many,)),
            pltpu.SemaphoreType.DMA((slots,)),
            pltpu.SemaphoreType.DMA((slots,)),
        ],
        compiler_params=pltpu.CompilerParams(collective_id=0, has_side_effects=True, vmem_limit_bytes=FULL_VMEM),
    )(
        counts.transpose(1, 0, 2),
        pair_mask.transpose(1, 2, 0, 3),
        coords.transpose(0, 2, 3, 1, 4),
        strain.transpose(1, 2, 0, 3),
        kappa_old.transpose(1, 2, 0, 3),
    )
    return kappa_new.transpose(2, 0, 1, 3), damage.transpose(2, 0, 1, 3)


def solution(mesh):
    placed = (
        P(None, "ply", "gx", "gy", None),
        P("ply", "gx", "gy", None),
        P("ply", "gx", "gy", None),
        P("ply", "gx", "gy"),
        P("ply", "gx", "gy", None),
    )
    sizes = tuple(mesh.shape[axis] for axis in AXES)
    return jax.shard_map(
        functools.partial(on_device, sizes),
        mesh=mesh,
        in_specs=placed,
        out_specs=(P("ply", "gx", "gy", None), P("ply", "gx", "gy", None)),
        check_vma=False,
    )
```

```python
import functools

import jax
import jax.numpy as jnp
from jax import lax
from jax.experimental import pallas as pl
from jax.experimental.pallas import tpu as pltpu
from jax.sharding import PartitionSpec as P

MESH = pl.DeviceIdType.MESH
AXES = ("ply", "gx", "gy")
FAR = -1e30
ROWS = 128
DEPTH = 32
AHEAD = 1
FULL_VMEM = 58 * 1024 * 1024


def directions():
    listed = []
    for layer in (0, 1):
        for dx in (-1, 0, 1):
            for dy in (-1, 0, 1):
                if (layer, dx, dy) != (0, 0, 0):
                    listed.append((layer, dx, dy))
    return listed


def send_span(step, size):
    return {-1: (1, 1), 0: (1, size), 1: (size, 1)}[step]


def land_span(step, size):
    return {-1: (0, 1), 0: (1, size), 1: (size + 1, 1)}[step]


def average_kernel(sizes, counts_in, mask_in, coords_in, strain_in, out_ref,
                   counts_ref, mask_ref, coords_ref, strain_ref, pack, source, target_side,
                   total_w, total_s, averaged, held, in_sem, send_sem, recv_sem, max_send, max_recv):
    across, along, _, points = strain_ref.shape
    wide, deep = across + 2, along + 2
    staged = [
        pltpu.make_async_copy(given, kept, in_sem.at[k])
        for k, (given, kept) in enumerate(
            [(counts_in, counts_ref), (coords_in, coords_ref), (strain_in, strain_ref), (mask_in, mask_ref)]
        )
    ]
    for copy in staged:
        copy.start()
    ply, gx, gy = (lax.axis_index(axis) for axis in AXES)
    listed = directions()

    def exists(dx, dy):
        x, y = gx + dx, gy + dy
        return (x >= 0) & (x < sizes[1]) & (y >= 0) & (y < sizes[2])

    def peer(layer, dx, dy):
        return (1 - ply if layer else ply, gx + dx, gy + dy)

    mine = ply * sizes[1] + gx
    first = sizes[0] * sizes[1]
    rounds = (
        [(1 + k, lax.rem(mine + 1 + k, first)) for k in range(first - 1)],
        [(1 + k, lax.rem(gy + 1 + k, sizes[2])) for k in range(sizes[2] - 1)],
    )

    def max_peer(which, index):
        return (index // sizes[1], lax.rem(index, sizes[1]), gy) if which == 0 else (ply, gx, index)

    pack[...] = jnp.zeros(pack.shape, jnp.float32)
    barrier = pltpu.get_barrier_semaphore()
    for layer, dx, dy in listed:
        @pl.when(exists(dx, dy))
        def _():
            pl.semaphore_signal(barrier, inc=1, device_id=peer(layer, dx, dy), device_id_type=MESH)
    for which in range(2):
        for _, index in rounds[which]:
            pl.semaphore_signal(barrier, inc=1, device_id=max_peer(which, index), device_id_type=MESH)

    slots = lax.broadcasted_iota(jnp.int32, (1, points), 1)
    for copy in staged[:3]:
        copy.wait()
    for x in range(across):
        for y in range(along):
            for comp in range(3):
                pack[0, x + 1, y + 1, pl.ds(comp, 1), :] = coords_ref[comp, x, y]
            live = slots < counts_ref[x, 0, y]
            pack[0, x + 1, y + 1, pl.ds(3, 1), :] = jnp.where(live, strain_ref[x, y], 0.0)

    wide_peers = 1 + (gx > 0).astype(jnp.int32) + (gx < sizes[1] - 1).astype(jnp.int32)
    deep_peers = 1 + (gy > 0).astype(jnp.int32) + (gy < sizes[2] - 1).astype(jnp.int32)
    pl.semaphore_wait(barrier, 2 * wide_peers * deep_peers - 1 + len(rounds[0]) + len(rounds[1]))

    def sending(which):
        layer, dx, dy = listed[which]
        (x0, nx), (y0, ny) = send_span(dx, across), send_span(dy, along)
        (u0, _), (v0, _) = land_span(-dx, across), land_span(-dy, along)
        return pltpu.make_async_remote_copy(
            src_ref=pack.at[0, pl.ds(x0, nx), pl.ds(y0, ny)],
            dst_ref=pack.at[layer, pl.ds(u0, nx), pl.ds(v0, ny)],
            send_sem=send_sem.at[which],
            recv_sem=recv_sem.at[which],
            device_id=peer(layer, dx, dy),
            device_id_type=MESH,
        )

    order = sorted(range(len(listed)), key=lambda which: (listed[which][1:] != (0, 0), -listed[which][0]))
    for which in order:
        @pl.when(exists(*listed[which][1:]))
        def _():
            sending(which).start()

    side = (1 - 2 * ply).astype(jnp.float32)
    sub = lax.broadcasted_iota(jnp.int32, (8, points), 0)
    top = sub < 4
    row = jnp.where(top, sub, sub - 4)
    last = jnp.where(top, 1.0, 0.0)

    def split(rows):
        high = rows.astype(jnp.bfloat16).astype(jnp.float32)
        rest = rows - high
        middle = rest.astype(jnp.bfloat16).astype(jnp.float32)
        return high, middle, rest - middle

    def spots(layer, x, y):
        origin = (layer * side - 0.5, x - 0.5 * wide, y - 0.5 * deep)
        found = [
            jnp.broadcast_to(pack[layer, x, y, pl.ds(comp, 1), :], (8, points)) + origin[comp] for comp in range(3)
        ]
        return found, found[0] * found[0] + found[1] * found[1] + found[2] * found[2]

    def stack(rows):
        return jnp.where(row == 0, rows[0], jnp.where(row == 1, rows[1], jnp.where(row == 2, rows[2], rows[3])))

    def build_source(layer, x, y, found, squared):
        strain = jnp.broadcast_to(pack[layer, x, y, pl.ds(3, 1), :], (8, points))
        high, middle, low = split(stack(found + [jnp.where(strain > 0.0, -squared, FAR)]))
        pair = jnp.where(top, high, middle)
        rows = jnp.concatenate([pair, jnp.where(top, high, low), pair, last], 0)
        source[layer, x, :, pl.ds(y * points, points)] = rows.astype(jnp.bfloat16)

    def build_target(x, y, found, squared):
        high, middle, low = split(stack([2.0 * spot for spot in found] + [jnp.ones((8, points), jnp.float32)]))
        a_high, a_middle, a_low = split(1.0 - squared)
        own = jnp.where(sub == 0, a_high, jnp.where(sub == 1, a_middle, jnp.where(sub == 2, a_low, jnp.where(sub == 4, 1.0, 0.0))))
        rows = jnp.concatenate([high, jnp.where(top, middle, high), jnp.where(top, low, middle), own], 0)
        target_side[(x - 1) * along + y - 1] = rows.T.astype(jnp.bfloat16)

    def own_row(x, carry):
        for y in range(1, along + 1):
            found, squared = spots(0, x, y)
            build_source(0, x, y, found, squared)
            build_target(x, y, found, squared)
        return carry

    lax.fori_loop(1, across + 1, own_row, 0)

    staged[3].wait()
    mask_base = jnp.where(ply == 0, 17, 0)

    half_rows = lax.broadcasted_iota(jnp.int32, (DEPTH // 2, points), 0)
    mask_row = jnp.where(half_rows == 12, 1.0, 0.0).astype(jnp.bfloat16)

    def masked_source(layer, x, y, near):
        block = source[layer, x + near // 3, :, pl.ds((y + near % 3) * points, points)]
        if layer == 0 and near == 4:
            return block
        flag = mask_ref[x, y, 0, mask_base + near if layer else 9 + near - (near > 4)]
        away = jnp.full(mask_row.shape, FAR * (1 - flag).astype(jnp.float32)).astype(jnp.bfloat16)
        return jnp.concatenate([block[: DEPTH // 2], block[DEPTH // 2 :] + mask_row * away], 0)

    def row_sums(x, ys, layer):
        tasks = [(y, at, pair) for y in ys for at in range(0, points, ROWS) for pair in range(0, 9, 2)]
        sides = {}

        def product(task):
            y, at, pair = task
            nears = [near for near in (pair, pair + 1) if near < 9]
            for near in nears:
                if (y, near) not in sides:
                    sides[y, near] = masked_source(layer, x, y, near)
            beside = jnp.concatenate([sides[y, near] for near in nears], axis=1)
            rows = target_side[x * along + y, pl.ds(at, ROWS), :]
            return nears, jnp.dot(rows, beside, preferred_element_type=jnp.float32)

        ready = [product(task) for task in tasks[:AHEAD]]
        sum_w = sum_s = None
        for k, (y, at, pair) in enumerate(tasks):
            if k + AHEAD < len(tasks):
                ready.append(product(tasks[k + AHEAD]))
            nears, inside = ready.pop(0)
            for slot, near in enumerate(nears):
                weight = jnp.maximum(inside[:, slot * points : (slot + 1) * points], 0.0)
                weight = weight * weight
                term = weight * pack[layer, x + near // 3, y + near % 3, pl.ds(3, 1), :]
                sum_w = weight if near == 0 else sum_w + weight
                sum_s = term if near == 0 else sum_s + term
            if pair == 8:
                place = (x * along + y, pl.ds(at, ROWS))
                if layer:
                    sum_w = sum_w + total_w[place]
                    sum_s = sum_s + total_s[place]
                total_w[place] = sum_w
                total_s[place] = sum_s

    def own_layer(x, ys):
        row_sums(x, ys, 0)

    def inner_row(x, carry):
        own_layer(x, range(1, along - 1))
        return carry

    lax.fori_loop(1, across - 1, inner_row, 0)

    for which in order:
        layer, dx, dy = listed[which]

        @pl.when(exists(dx, dy))
        def _():
            (u0, nx), (v0, ny) = land_span(dx, across), land_span(dy, along)
            (x0, _), (y0, _) = send_span(dx, across), send_span(dy, along)
            arriving = pltpu.make_async_remote_copy(
                src_ref=pack.at[0, pl.ds(x0, nx), pl.ds(y0, ny)],
                dst_ref=pack.at[layer, pl.ds(u0, nx), pl.ds(v0, ny)],
                send_sem=send_sem.at[which],
                recv_sem=recv_sem.at[listed.index((layer, -dx, -dy))],
                device_id=peer(layer, dx, dy),
                device_id_type=MESH,
            )
            arriving.wait_recv()
            sending(which).wait_send()

    def halo_row(x, carry):
        for y in range(deep):
            build_source(1, x, y, *spots(1, x, y))
        for y in (0, deep - 1):
            build_source(0, x, y, *spots(0, x, y))
        return carry

    def halo_end(end, carry):
        x = end * (wide - 1)
        for y in range(1, deep - 1):
            build_source(0, x, y, *spots(0, x, y))
        return carry

    lax.fori_loop(0, wide, halo_row, 0)
    lax.fori_loop(0, 2, halo_end, 0)

    def edge_row(x, carry):
        own_layer(x, (0, along - 1))
        return carry

    def end_row(end, carry):
        own_layer(end * (across - 1), range(along))
        return carry

    lax.fori_loop(1, across - 1, edge_row, 0)
    lax.fori_loop(0, 2, end_row, 0)

    def other_layer(x, carry):
        row_sums(x, range(along), 1)
        return carry

    lax.fori_loop(0, across, other_layer, 0)

    ones = jnp.ones((8, 2 * points), jnp.bfloat16)

    def lane_sums(block):
        high = block.astype(jnp.bfloat16)
        low = (block - high.astype(jnp.float32)).astype(jnp.bfloat16)
        both = jnp.concatenate([high, low], axis=1)
        summed = lax.dot_general(ones, both, (((1,), (1,)), ((), ())), preferred_element_type=jnp.float32)
        return summed[0:1]

    def divide(x, carry):
        these = pl.ds(x * along, along)
        weight_sum = lane_sums(total_w[these].reshape(along * points, points))
        weighted = lane_sums(total_s[these].reshape(along * points, points))
        for y in range(along):
            span = slice(y * points, (y + 1) * points)
            live = slots < counts_ref[x, 0, y]
            share = weighted[:, span] / jnp.where(live, weight_sum[:, span], 1.0)
            averaged[x, pl.ds(y, 1), :] = jnp.where(live, share, 0.0)
        return carry

    lax.fori_loop(0, across, divide, 0)

    best = jnp.max(averaged[...])
    at = 0
    for which in range(2):
        held[at] = jnp.full(held.shape[1:], best, jnp.float32)
        copies = []
        for step, index in rounds[which]:
            copies.append(
                pltpu.make_async_remote_copy(
                    src_ref=held.at[at],
                    dst_ref=held.at[at + step],
                    send_sem=max_send.at[at + step],
                    recv_sem=max_recv.at[at + step],
                    device_id=max_peer(which, index),
                    device_id_type=MESH,
                )
            )
        for copy in copies:
            copy.start()
        for copy in copies:
            copy.wait()
        best = held[at]
        for step, _ in rounds[which]:
            best = jnp.maximum(best, held[at + step])
        best = best if which else jnp.max(best)
        at += len(rounds[which]) + 1

    highest = best[0:1] + 1e-06
    for x in range(across):
        for y in range(along):
            scaled = 4.0 * averaged[x, pl.ds(y, 1), :] / highest
            out_ref[x, y] = jnp.where(slots < counts_ref[x, 0, y], scaled, -1.0)


def on_device(sizes, coords, strain, kappa_old, counts, pair_mask):
    layers, across, along, points = strain.shape
    assert layers == 1 and sizes[0] == 2
    wide, deep = across + 2, along + 2
    vmem = pl.BlockSpec(memory_space=pltpu.VMEM)
    many = len(directions())
    targets = across * along
    slots = sizes[0] * sizes[1] + sizes[2]
    scaled = pl.pallas_call(
        functools.partial(average_kernel, sizes),
        out_shape=jax.ShapeDtypeStruct((across, along, 1, points), jnp.float32),
        in_specs=[pl.BlockSpec(memory_space=pl.ANY)] * 4,
        out_specs=vmem,
        scratch_shapes=[
            pltpu.SMEM((across, 1, along), jnp.int32),
            pltpu.SMEM((across, along, 1, pair_mask.shape[3]), jnp.int32),
            pltpu.VMEM((3, across, along, 1, points), jnp.float32),
            pltpu.VMEM((across, along, 1, points), jnp.float32),
            pltpu.VMEM((2, wide, deep, 4, points), jnp.float32),
            pltpu.VMEM((2, wide, DEPTH, deep * points), jnp.bfloat16),
            pltpu.VMEM((targets, points, DEPTH), jnp.bfloat16),
            pltpu.VMEM((targets, points, points), jnp.float32),
            pltpu.VMEM((targets, points, points), jnp.float32),
            pltpu.VMEM((across, along, points), jnp.float32),
            pltpu.VMEM((slots, 8, points), jnp.float32),
            pltpu.SemaphoreType.DMA((4,)),
            pltpu.SemaphoreType.DMA((many,)),
            pltpu.SemaphoreType.DMA((many,)),
            pltpu.SemaphoreType.DMA((slots,)),
            pltpu.SemaphoreType.DMA((slots,)),
        ],
        compiler_params=pltpu.CompilerParams(collective_id=0, has_side_effects=True, vmem_limit_bytes=FULL_VMEM),
    )(
        counts.transpose(1, 0, 2),
        pair_mask.transpose(1, 2, 0, 3),
        coords.transpose(0, 2, 3, 1, 4),
        strain.transpose(1, 2, 0, 3),
    )
    scaled = scaled.transpose(2, 0, 1, 3)
    kappa_new = jnp.maximum(kappa_old, scaled)
    damage = jnp.where(scaled < 0.0, 0.0, 1.0 - jnp.exp(-(kappa_new - 1.0) / 2.5) / kappa_new)
    return kappa_new, damage


def solution(mesh):
    placed = (
        P(None, "ply", "gx", "gy", None),
        P("ply", "gx", "gy", None),
        P("ply", "gx", "gy", None),
        P("ply", "gx", "gy"),
        P("ply", "gx", "gy", None),
    )
    sizes = tuple(mesh.shape[axis] for axis in AXES)
    return jax.shard_map(
        functools.partial(on_device, sizes),
        mesh=mesh,
        in_specs=placed,
        out_specs=(P("ply", "gx", "gy", None), P("ply", "gx", "gy", None)),
        check_vma=False,
    )
```

```python
import functools

import jax
import jax.numpy as jnp
from jax import lax
from jax.experimental import pallas as pl
from jax.experimental.pallas import tpu as pltpu
from jax.sharding import PartitionSpec as P

MESH = pl.DeviceIdType.MESH
AXES = ("ply", "gx", "gy")
FAR = -1e30
CHUNK = 32
DEPTH = 32
AHEAD = 1
FULL_VMEM = 58 * 1024 * 1024


def directions():
    listed = []
    for layer in (0, 1):
        for dx in (-1, 0, 1):
            for dy in (-1, 0, 1):
                if (layer, dx, dy) != (0, 0, 0):
                    listed.append((layer, dx, dy))
    return listed


def send_span(step, size):
    return {-1: (1, 1), 0: (1, size), 1: (size, 1)}[step]


def land_span(step, size):
    return {-1: (0, 1), 0: (1, size), 1: (size + 1, 1)}[step]


def average_kernel(sizes, counts_in, mask_in, coords_in, strain_in, out_ref,
                   counts_ref, mask_ref, coords_ref, strain_ref, pack, plain, source, target_side, column,
                   total_w, total_s, averaged, held, in_sem, send_sem, recv_sem, max_send, max_recv):
    across, along, _, points = strain_ref.shape
    wide, deep = across + 2, along + 2
    staged = [
        pltpu.make_async_copy(given, kept, in_sem.at[k])
        for k, (given, kept) in enumerate(
            [(counts_in, counts_ref), (coords_in, coords_ref), (strain_in, strain_ref), (mask_in, mask_ref)]
        )
    ]
    for copy in staged:
        copy.start()
    ply, gx, gy = (lax.axis_index(axis) for axis in AXES)
    listed = directions()

    def exists(dx, dy):
        x, y = gx + dx, gy + dy
        return (x >= 0) & (x < sizes[1]) & (y >= 0) & (y < sizes[2])

    def peer(layer, dx, dy):
        return (1 - ply if layer else ply, gx + dx, gy + dy)

    mine = ply * sizes[1] + gx
    first = sizes[0] * sizes[1]
    rounds = (
        [(1 + k, lax.rem(mine + 1 + k, first)) for k in range(first - 1)],
        [(1 + k, lax.rem(gy + 1 + k, sizes[2])) for k in range(sizes[2] - 1)],
    )

    def max_peer(which, index):
        return (index // sizes[1], lax.rem(index, sizes[1]), gy) if which == 0 else (ply, gx, index)

    pack[...] = jnp.zeros(pack.shape, jnp.float32)
    barrier = pltpu.get_barrier_semaphore()
    for layer, dx, dy in listed:
        @pl.when(exists(dx, dy))
        def _():
            pl.semaphore_signal(barrier, inc=1, device_id=peer(layer, dx, dy), device_id_type=MESH)
    for which in range(2):
        for _, index in rounds[which]:
            pl.semaphore_signal(barrier, inc=1, device_id=max_peer(which, index), device_id_type=MESH)

    slots = lax.broadcasted_iota(jnp.int32, (1, points), 1)
    for copy in staged[:3]:
        copy.wait()
    for x in range(across):
        for y in range(along):
            for comp in range(3):
                pack[0, x + 1, y + 1, pl.ds(comp, 1), :] = coords_ref[comp, x, y]
            live = slots < counts_ref[x, 0, y]
            pack[0, x + 1, y + 1, pl.ds(3, 1), :] = jnp.where(live, strain_ref[x, y], 0.0)

    wide_peers = 1 + (gx > 0).astype(jnp.int32) + (gx < sizes[1] - 1).astype(jnp.int32)
    deep_peers = 1 + (gy > 0).astype(jnp.int32) + (gy < sizes[2] - 1).astype(jnp.int32)
    pl.semaphore_wait(barrier, 2 * wide_peers * deep_peers - 1 + len(rounds[0]) + len(rounds[1]))

    def sending(which):
        layer, dx, dy = listed[which]
        (x0, nx), (y0, ny) = send_span(dx, across), send_span(dy, along)
        (u0, _), (v0, _) = land_span(-dx, across), land_span(-dy, along)
        return pltpu.make_async_remote_copy(
            src_ref=pack.at[0, pl.ds(x0, nx), pl.ds(y0, ny)],
            dst_ref=pack.at[layer, pl.ds(u0, nx), pl.ds(v0, ny)],
            send_sem=send_sem.at[which],
            recv_sem=recv_sem.at[which],
            device_id=peer(layer, dx, dy),
            device_id_type=MESH,
        )

    order = sorted(range(len(listed)), key=lambda which: (listed[which][1:] != (0, 0), -listed[which][0]))
    for which in order:
        @pl.when(exists(*listed[which][1:]))
        def _():
            sending(which).start()

    side = (1 - 2 * ply).astype(jnp.float32)
    sub = lax.broadcasted_iota(jnp.int32, (8, points), 0)
    top = sub < 4
    row = jnp.where(top, sub, sub - 4)
    last = jnp.where(top, 1.0, 0.0)

    def split(rows):
        high = rows.astype(jnp.bfloat16).astype(jnp.float32)
        rest = rows - high
        middle = rest.astype(jnp.bfloat16).astype(jnp.float32)
        return high, middle, rest - middle

    def spots(layer, x, y):
        origin = (layer * side - 0.5, x - 0.5 * wide, y - 0.5 * deep)
        found = [
            jnp.broadcast_to(pack[layer, x, y, pl.ds(comp, 1), :], (8, points)) + origin[comp] for comp in range(3)
        ]
        return found, found[0] * found[0] + found[1] * found[1] + found[2] * found[2]

    def stack(rows):
        return jnp.where(row == 0, rows[0], jnp.where(row == 1, rows[1], jnp.where(row == 2, rows[2], rows[3])))

    def build_source(layer, x, y, found, squared):
        strain = jnp.broadcast_to(pack[layer, x, y, pl.ds(3, 1), :], (8, points))
        rows = stack(found + [jnp.where(strain > 0.0, -squared, FAR)])
        plain[layer, x, y] = rows[:4]
        high, middle, low = split(rows)
        pair = jnp.where(top, high, middle)
        rows = jnp.concatenate([pair, jnp.where(top, high, low), pair, last], 0)
        source[layer, x, :, pl.ds(y * points, points)] = rows.astype(jnp.bfloat16)

    def build_target(x, y, found, squared):
        high, middle, low = split(stack([2.0 * spot for spot in found] + [jnp.ones((8, points), jnp.float32)]))
        a_high, a_middle, a_low = split(1.0 - squared)
        own = jnp.where(sub == 0, a_high, jnp.where(sub == 1, a_middle, jnp.where(sub == 2, a_low, jnp.where(sub == 4, 1.0, 0.0))))
        twice = stack([2.0 * spot for spot in found] + [1.0 - squared])
        rows = jnp.concatenate([high, jnp.where(top, middle, high), jnp.where(top, low, middle), own, twice], 0).T
        target = (x - 1) * along + y - 1
        target_side[target] = rows[:, :DEPTH].astype(jnp.bfloat16)
        for comp in range(4):
            column[target, comp] = jnp.broadcast_to(rows[:, DEPTH + comp : DEPTH + comp + 1], (points, points))

    def own_row(x, carry):
        for y in range(1, along + 1):
            found, squared = spots(0, x, y)
            build_source(0, x, y, found, squared)
            build_target(x, y, found, squared)
        return carry

    lax.fori_loop(1, across + 1, own_row, 0)

    staged[3].wait()
    mask_base = jnp.where(ply == 0, 17, 0)

    half_rows = lax.broadcasted_iota(jnp.int32, (DEPTH // 2, points), 0)
    mask_row = jnp.where(half_rows == 12, 1.0, 0.0).astype(jnp.bfloat16)

    def away_from(layer, x, y, near):
        flag = mask_ref[x, y, 0, mask_base + near if layer else 9 + near - (near > 4)]
        return FAR * (1 - flag).astype(jnp.float32)

    def masked_source(layer, x, y, near):
        block = source[layer, x + near // 3, :, pl.ds((y + near % 3) * points, points)]
        if layer == 0 and near == 4:
            return block
        away = jnp.full(mask_row.shape, away_from(layer, x, y, near)).astype(jnp.bfloat16)
        return jnp.concatenate([block[: DEPTH // 2], block[DEPTH // 2 :] + mask_row * away], 0)

    def row_sums(x, ys, layer):
        tasks = [(y, step) for y in ys for step in range(3)]

        def product(task):
            y, step = task
            beside = jnp.concatenate([masked_source(layer, x, y, 3 * step + slot) for slot in range(2)], axis=1)
            return jnp.dot(target_side[x * along + y], beside, preferred_element_type=jnp.float32)

        def add(at, inside, near, y):
            weight = jnp.maximum(inside, 0.0)
            weight = weight * weight
            term = weight * pack[layer, x + near // 3, y + near % 3, pl.ds(3, 1), :]
            sums[at] = (sums[at][0] + weight, sums[at][1] + term) if at in sums else (weight, term)

        def direct(at, y):
            spot = [column[x * along + y, comp, pl.ds(at, CHUNK), :] for comp in range(4)]
            for near in (2, 5, 8):
                row = [plain[layer, x + near // 3, y + 2, pl.ds(comp, 1), :] for comp in range(4)]
                fixed = row[3] + away_from(layer, x, y, near)
                add(at, spot[0] * row[0] + spot[1] * row[1] + (spot[2] * row[2] + (spot[3] + fixed)), near, y)

        spans = range(0, points, CHUNK)
        ready = [product(task) for task in tasks[:AHEAD]]
        for k, (y, step) in enumerate(tasks):
            if step == 0:
                sums = {}
            if k + AHEAD < len(tasks):
                ready.append(product(tasks[k + AHEAD]))
            for at in list(spans)[step :: 3]:
                direct(at, y)
            inside = ready.pop(0)
            for at in spans:
                for slot in range(2):
                    add(at, inside[at : at + CHUNK, slot * points : (slot + 1) * points], 3 * step + slot, y)
            if step == 2:
                for at in spans:
                    place = (x * along + y, pl.ds(at, CHUNK))
                    sum_w, sum_s = sums[at]
                    if layer:
                        sum_w = sum_w + total_w[place]
                        sum_s = sum_s + total_s[place]
                    total_w[place] = sum_w
                    total_s[place] = sum_s

    def own_layer(x, ys):
        row_sums(x, ys, 0)

    def inner_row(x, carry):
        own_layer(x, range(1, along - 1))
        return carry

    lax.fori_loop(1, across - 1, inner_row, 0)

    for which in order:
        layer, dx, dy = listed[which]

        @pl.when(exists(dx, dy))
        def _():
            (u0, nx), (v0, ny) = land_span(dx, across), land_span(dy, along)
            (x0, _), (y0, _) = send_span(dx, across), send_span(dy, along)
            arriving = pltpu.make_async_remote_copy(
                src_ref=pack.at[0, pl.ds(x0, nx), pl.ds(y0, ny)],
                dst_ref=pack.at[layer, pl.ds(u0, nx), pl.ds(v0, ny)],
                send_sem=send_sem.at[which],
                recv_sem=recv_sem.at[listed.index((layer, -dx, -dy))],
                device_id=peer(layer, dx, dy),
                device_id_type=MESH,
            )
            arriving.wait_recv()
            sending(which).wait_send()

    def halo_row(x, carry):
        for y in range(deep):
            build_source(1, x, y, *spots(1, x, y))
        for y in (0, deep - 1):
            build_source(0, x, y, *spots(0, x, y))
        return carry

    def halo_end(end, carry):
        x = end * (wide - 1)
        for y in range(1, deep - 1):
            build_source(0, x, y, *spots(0, x, y))
        return carry

    lax.fori_loop(0, wide, halo_row, 0)
    lax.fori_loop(0, 2, halo_end, 0)

    def edge_row(x, carry):
        own_layer(x, (0, along - 1))
        return carry

    def end_row(end, carry):
        own_layer(end * (across - 1), range(along))
        return carry

    lax.fori_loop(1, across - 1, edge_row, 0)
    lax.fori_loop(0, 2, end_row, 0)

    def other_layer(x, carry):
        row_sums(x, range(along), 1)
        return carry

    lax.fori_loop(0, across, other_layer, 0)

    ones = jnp.ones((8, 2 * points), jnp.bfloat16)

    def lane_sums(block):
        high = block.astype(jnp.bfloat16)
        low = (block - high.astype(jnp.float32)).astype(jnp.bfloat16)
        both = jnp.concatenate([high, low], axis=1)
        summed = lax.dot_general(ones, both, (((1,), (1,)), ((), ())), preferred_element_type=jnp.float32)
        return summed[0:1]

    def divide(x, carry):
        these = pl.ds(x * along, along)
        weight_sum = lane_sums(total_w[these].reshape(along * points, points))
        weighted = lane_sums(total_s[these].reshape(along * points, points))
        for y in range(along):
            span = slice(y * points, (y + 1) * points)
            live = slots < counts_ref[x, 0, y]
            share = weighted[:, span] / jnp.where(live, weight_sum[:, span], 1.0)
            averaged[x, pl.ds(y, 1), :] = jnp.where(live, share, 0.0)
        return carry

    lax.fori_loop(0, across, divide, 0)

    best = jnp.max(averaged[...])
    at = 0
    for which in range(2):
        held[at] = jnp.full(held.shape[1:], best, jnp.float32)
        copies = []
        for step, index in rounds[which]:
            copies.append(
                pltpu.make_async_remote_copy(
                    src_ref=held.at[at],
                    dst_ref=held.at[at + step],
                    send_sem=max_send.at[at + step],
                    recv_sem=max_recv.at[at + step],
                    device_id=max_peer(which, index),
                    device_id_type=MESH,
                )
            )
        for copy in copies:
            copy.start()
        for copy in copies:
            copy.wait()
        best = held[at]
        for step, _ in rounds[which]:
            best = jnp.maximum(best, held[at + step])
        best = best if which else jnp.max(best)
        at += len(rounds[which]) + 1

    highest = best[0:1] + 1e-06
    for x in range(across):
        for y in range(along):
            scaled = 4.0 * averaged[x, pl.ds(y, 1), :] / highest
            out_ref[x, y] = jnp.where(slots < counts_ref[x, 0, y], scaled, -1.0)


def on_device(sizes, coords, strain, kappa_old, counts, pair_mask):
    layers, across, along, points = strain.shape
    assert layers == 1 and sizes[0] == 2
    wide, deep = across + 2, along + 2
    vmem = pl.BlockSpec(memory_space=pltpu.VMEM)
    many = len(directions())
    targets = across * along
    slots = sizes[0] * sizes[1] + sizes[2]
    scaled = pl.pallas_call(
        functools.partial(average_kernel, sizes),
        out_shape=jax.ShapeDtypeStruct((across, along, 1, points), jnp.float32),
        in_specs=[pl.BlockSpec(memory_space=pl.ANY)] * 4,
        out_specs=vmem,
        scratch_shapes=[
            pltpu.SMEM((across, 1, along), jnp.int32),
            pltpu.SMEM((across, along, 1, pair_mask.shape[3]), jnp.int32),
            pltpu.VMEM((3, across, along, 1, points), jnp.float32),
            pltpu.VMEM((across, along, 1, points), jnp.float32),
            pltpu.VMEM((2, wide, deep, 4, points), jnp.float32),
            pltpu.VMEM((2, wide, deep, 4, points), jnp.float32),
            pltpu.VMEM((2, wide, DEPTH, deep * points), jnp.bfloat16),
            pltpu.VMEM((targets, points, DEPTH), jnp.bfloat16),
            pltpu.VMEM((targets, 4, points, points), jnp.float32),
            pltpu.VMEM((targets, points, points), jnp.float32),
            pltpu.VMEM((targets, points, points), jnp.float32),
            pltpu.VMEM((across, along, points), jnp.float32),
            pltpu.VMEM((slots, 8, points), jnp.float32),
            pltpu.SemaphoreType.DMA((4,)),
            pltpu.SemaphoreType.DMA((many,)),
            pltpu.SemaphoreType.DMA((many,)),
            pltpu.SemaphoreType.DMA((slots,)),
            pltpu.SemaphoreType.DMA((slots,)),
        ],
        compiler_params=pltpu.CompilerParams(collective_id=0, has_side_effects=True, vmem_limit_bytes=FULL_VMEM),
    )(
        counts.transpose(1, 0, 2),
        pair_mask.transpose(1, 2, 0, 3),
        coords.transpose(0, 2, 3, 1, 4),
        strain.transpose(1, 2, 0, 3),
    )
    scaled = scaled.transpose(2, 0, 1, 3)
    kappa_new = jnp.maximum(kappa_old, scaled)
    damage = jnp.where(scaled < 0.0, 0.0, 1.0 - jnp.exp(-(kappa_new - 1.0) / 2.5) / kappa_new)
    return kappa_new, damage


def solution(mesh):
    placed = (
        P(None, "ply", "gx", "gy", None),
        P("ply", "gx", "gy", None),
        P("ply", "gx", "gy", None),
        P("ply", "gx", "gy"),
        P("ply", "gx", "gy", None),
    )
    sizes = tuple(mesh.shape[axis] for axis in AXES)
    return jax.shard_map(
        functools.partial(on_device, sizes),
        mesh=mesh,
        in_specs=placed,
        out_specs=(P("ply", "gx", "gy", None), P("ply", "gx", "gy", None)),
        check_vma=False,
    )
```

```python
import functools

import jax
import jax.numpy as jnp
from jax import lax
from jax.experimental import pallas as pl
from jax.experimental.pallas import tpu as pltpu
from jax.sharding import PartitionSpec as P

MESH = pl.DeviceIdType.MESH
AXES = ("ply", "gx", "gy")
FAR = -1e30
ROWS = 32
DEPTH = 32
AHEAD = 1
FULL_VMEM = 58 * 1024 * 1024


def directions():
    listed = []
    for layer in (0, 1):
        for dx in (-1, 0, 1):
            for dy in (-1, 0, 1):
                if (layer, dx, dy) != (0, 0, 0):
                    listed.append((layer, dx, dy))
    return listed


def send_span(step, size):
    return {-1: (1, 1), 0: (1, size), 1: (size, 1)}[step]


def land_span(step, size):
    return {-1: (0, 1), 0: (1, size), 1: (size + 1, 1)}[step]


def average_kernel(sizes, counts_in, mask_in, coords_in, strain_in, out_ref,
                   counts_ref, mask_ref, coords_ref, strain_ref, pack, source, target_side,
                   total_w, total_s, averaged, held, in_sem, send_sem, recv_sem, max_send, max_recv):
    across, along, _, points = strain_ref.shape
    wide, deep = across + 2, along + 2
    staged = [
        pltpu.make_async_copy(given, kept, in_sem.at[k])
        for k, (given, kept) in enumerate(
            [(counts_in, counts_ref), (coords_in, coords_ref), (strain_in, strain_ref), (mask_in, mask_ref)]
        )
    ]
    for copy in staged:
        copy.start()
    ply, gx, gy = (lax.axis_index(axis) for axis in AXES)
    listed = directions()

    def exists(dx, dy):
        x, y = gx + dx, gy + dy
        return (x >= 0) & (x < sizes[1]) & (y >= 0) & (y < sizes[2])

    def peer(layer, dx, dy):
        return (1 - ply if layer else ply, gx + dx, gy + dy)

    mine = ply * sizes[1] + gx
    first = sizes[0] * sizes[1]
    rounds = (
        [(1 + k, lax.rem(mine + 1 + k, first)) for k in range(first - 1)],
        [(1 + k, lax.rem(gy + 1 + k, sizes[2])) for k in range(sizes[2] - 1)],
    )

    def max_peer(which, index):
        return (index // sizes[1], lax.rem(index, sizes[1]), gy) if which == 0 else (ply, gx, index)

    pack[...] = jnp.zeros(pack.shape, jnp.float32)
    barrier = pltpu.get_barrier_semaphore()
    for layer, dx, dy in listed:
        @pl.when(exists(dx, dy))
        def _():
            pl.semaphore_signal(barrier, inc=1, device_id=peer(layer, dx, dy), device_id_type=MESH)
    for which in range(2):
        for _, index in rounds[which]:
            pl.semaphore_signal(barrier, inc=1, device_id=max_peer(which, index), device_id_type=MESH)

    slots = lax.broadcasted_iota(jnp.int32, (1, points), 1)
    for copy in staged[:3]:
        copy.wait()
    for x in range(across):
        for y in range(along):
            for comp in range(3):
                pack[0, x + 1, y + 1, pl.ds(comp, 1), :] = coords_ref[comp, x, y]
            live = slots < counts_ref[x, 0, y]
            pack[0, x + 1, y + 1, pl.ds(3, 1), :] = jnp.where(live, strain_ref[x, y], 0.0)

    wide_peers = 1 + (gx > 0).astype(jnp.int32) + (gx < sizes[1] - 1).astype(jnp.int32)
    deep_peers = 1 + (gy > 0).astype(jnp.int32) + (gy < sizes[2] - 1).astype(jnp.int32)
    pl.semaphore_wait(barrier, 2 * wide_peers * deep_peers - 1 + len(rounds[0]) + len(rounds[1]))

    def sending(which):
        layer, dx, dy = listed[which]
        (x0, nx), (y0, ny) = send_span(dx, across), send_span(dy, along)
        (u0, _), (v0, _) = land_span(-dx, across), land_span(-dy, along)
        return pltpu.make_async_remote_copy(
            src_ref=pack.at[0, pl.ds(x0, nx), pl.ds(y0, ny)],
            dst_ref=pack.at[layer, pl.ds(u0, nx), pl.ds(v0, ny)],
            send_sem=send_sem.at[which],
            recv_sem=recv_sem.at[which],
            device_id=peer(layer, dx, dy),
            device_id_type=MESH,
        )

    order = sorted(range(len(listed)), key=lambda which: (listed[which][1:] != (0, 0), -listed[which][0]))
    for which in order:
        @pl.when(exists(*listed[which][1:]))
        def _():
            sending(which).start()

    side = (1 - 2 * ply).astype(jnp.float32)
    sub = lax.broadcasted_iota(jnp.int32, (8, points), 0)
    top = sub < 4
    row = jnp.where(top, sub, sub - 4)
    last = jnp.where(top, 1.0, 0.0)

    def split(rows):
        high = rows.astype(jnp.bfloat16).astype(jnp.float32)
        rest = rows - high
        middle = rest.astype(jnp.bfloat16).astype(jnp.float32)
        return high, middle, rest - middle

    def spots(layer, x, y):
        origin = (layer * side - 0.5, x - 0.5 * wide, y - 0.5 * deep)
        found = [
            jnp.broadcast_to(pack[layer, x, y, pl.ds(comp, 1), :], (8, points)) + origin[comp] for comp in range(3)
        ]
        return found, found[0] * found[0] + found[1] * found[1] + found[2] * found[2]

    def stack(rows):
        return jnp.where(row == 0, rows[0], jnp.where(row == 1, rows[1], jnp.where(row == 2, rows[2], rows[3])))

    def build_source(layer, x, y, found, squared):
        strain = jnp.broadcast_to(pack[layer, x, y, pl.ds(3, 1), :], (8, points))
        high, middle, low = split(stack(found + [jnp.where(strain > 0.0, -squared, FAR)]))
        pair = jnp.where(top, high, middle)
        rows = jnp.concatenate([pair, jnp.where(top, high, low), pair, last], 0)
        source[layer, x, :, pl.ds(y * points, points)] = rows.astype(jnp.bfloat16)

    def build_target(x, y, found, squared):
        high, middle, low = split(stack([2.0 * spot for spot in found] + [jnp.ones((8, points), jnp.float32)]))
        a_high, a_middle, a_low = split(1.0 - squared)
        own = jnp.where(sub == 0, a_high, jnp.where(sub == 1, a_middle, jnp.where(sub == 2, a_low, jnp.where(sub == 4, 1.0, 0.0))))
        rows = jnp.concatenate([high, jnp.where(top, middle, high), jnp.where(top, low, middle), own], 0)
        target_side[(x - 1) * along + y - 1] = rows.T.astype(jnp.bfloat16)

    def own_row(x, carry):
        for y in range(1, along + 1):
            found, squared = spots(0, x, y)
            build_source(0, x, y, found, squared)
            build_target(x, y, found, squared)
        return carry

    lax.fori_loop(1, across + 1, own_row, 0, unroll=2)

    staged[3].wait()
    mask_base = jnp.where(ply == 0, 17, 0)

    half_rows = lax.broadcasted_iota(jnp.int32, (DEPTH // 2, points), 0)
    mask_row = jnp.where(half_rows == 12, 1.0, 0.0).astype(jnp.bfloat16)

    def masked_source(layer, x, y, near):
        block = source[layer, x + near // 3, :, pl.ds((y + near % 3) * points, points)]
        if layer == 0 and near == 4:
            return block
        flag = mask_ref[x, y, 0, mask_base + near if layer else 9 + near - (near > 4)]
        away = jnp.full(mask_row.shape, FAR * (1 - flag).astype(jnp.float32)).astype(jnp.bfloat16)
        return jnp.concatenate([block[: DEPTH // 2], block[DEPTH // 2 :] + mask_row * away], 0)

    def row_sums(x, ys, layer):
        def product(y):
            beside = jnp.concatenate([masked_source(layer, x, y, near) for near in range(9)], axis=1)
            return jnp.dot(target_side[x * along + y], beside, preferred_element_type=jnp.float32)

        ready = [product(y) for y in ys[:AHEAD]]
        for k, y in enumerate(ys):
            if k + AHEAD < len(ys):
                ready.append(product(ys[k + AHEAD]))
            inside = ready.pop(0)
            for at in range(0, points, ROWS):
                sum_w = sum_s = None
                for near in range(9):
                    weight = jnp.maximum(inside[at : at + ROWS, near * points : (near + 1) * points], 0.0)
                    weight = weight * weight
                    term = weight * pack[layer, x + near // 3, y + near % 3, pl.ds(3, 1), :]
                    sum_w = weight if near == 0 else sum_w + weight
                    sum_s = term if near == 0 else sum_s + term
                place = (x * along + y, pl.ds(at, ROWS))
                if layer:
                    sum_w = sum_w + total_w[place]
                    sum_s = sum_s + total_s[place]
                total_w[place] = sum_w
                total_s[place] = sum_s

    def own_layer(x, ys):
        row_sums(x, ys, 0)

    def inner_row(x, carry):
        own_layer(x, range(1, along - 1))
        return carry

    lax.fori_loop(1, across - 1, inner_row, 0)

    for which in order:
        layer, dx, dy = listed[which]

        @pl.when(exists(dx, dy))
        def _():
            (u0, nx), (v0, ny) = land_span(dx, across), land_span(dy, along)
            (x0, _), (y0, _) = send_span(dx, across), send_span(dy, along)
            arriving = pltpu.make_async_remote_copy(
                src_ref=pack.at[0, pl.ds(x0, nx), pl.ds(y0, ny)],
                dst_ref=pack.at[layer, pl.ds(u0, nx), pl.ds(v0, ny)],
                send_sem=send_sem.at[which],
                recv_sem=recv_sem.at[listed.index((layer, -dx, -dy))],
                device_id=peer(layer, dx, dy),
                device_id_type=MESH,
            )
            arriving.wait_recv()
            sending(which).wait_send()

    def halo_row(x, carry):
        for y in range(deep):
            build_source(1, x, y, *spots(1, x, y))
        for y in (0, deep - 1):
            build_source(0, x, y, *spots(0, x, y))
        return carry

    def halo_end(end, carry):
        x = end * (wide - 1)
        for y in range(1, deep - 1):
            build_source(0, x, y, *spots(0, x, y))
        return carry

    lax.fori_loop(0, wide, halo_row, 0, unroll=2)
    lax.fori_loop(0, 2, halo_end, 0, unroll=2)

    def edge_row(x, carry):
        own_layer(x, (0, along - 1))
        return carry

    def end_row(end, carry):
        own_layer(end * (across - 1), range(along))
        return carry

    lax.fori_loop(1, across - 1, edge_row, 0)
    lax.fori_loop(0, 2, end_row, 0)

    def other_layer(x, carry):
        row_sums(x, range(along), 1)
        return carry

    lax.fori_loop(0, across, other_layer, 0)

    ones = jnp.ones((8, 2 * points), jnp.bfloat16)

    def lane_sums(block):
        high = block.astype(jnp.bfloat16)
        low = (block - high.astype(jnp.float32)).astype(jnp.bfloat16)
        both = jnp.concatenate([high, low], axis=1)
        summed = lax.dot_general(ones, both, (((1,), (1,)), ((), ())), preferred_element_type=jnp.float32)
        return summed[0:1]

    def divide(x, carry):
        these = pl.ds(x * along, along)
        weight_sum = lane_sums(total_w[these].reshape(along * points, points))
        weighted = lane_sums(total_s[these].reshape(along * points, points))
        for y in range(along):
            span = slice(y * points, (y + 1) * points)
            live = slots < counts_ref[x, 0, y]
            share = weighted[:, span] / jnp.where(live, weight_sum[:, span], 1.0)
            averaged[x, pl.ds(y, 1), :] = jnp.where(live, share, 0.0)
        return carry

    for x in range(across):
        divide(x, 0)

    best = jnp.max(averaged[...])
    at = 0
    for which in range(2):
        held[at] = jnp.full(held.shape[1:], best, jnp.float32)
        copies = []
        for step, index in rounds[which]:
            copies.append(
                pltpu.make_async_remote_copy(
                    src_ref=held.at[at],
                    dst_ref=held.at[at + step],
                    send_sem=max_send.at[at + step],
                    recv_sem=max_recv.at[at + step],
                    device_id=max_peer(which, index),
                    device_id_type=MESH,
                )
            )
        for copy in copies:
            copy.start()
        for copy in copies:
            copy.wait()
        best = held[at]
        for step, _ in rounds[which]:
            best = jnp.maximum(best, held[at + step])
        best = best if which else jnp.max(best)
        at += len(rounds[which]) + 1

    highest = best[0:1] + 1e-06
    for x in range(across):
        for y in range(along):
            scaled = 4.0 * averaged[x, pl.ds(y, 1), :] / highest
            out_ref[x, y] = jnp.where(slots < counts_ref[x, 0, y], scaled, -1.0)


def on_device(sizes, coords, strain, kappa_old, counts, pair_mask):
    layers, across, along, points = strain.shape
    assert layers == 1 and sizes[0] == 2
    wide, deep = across + 2, along + 2
    vmem = pl.BlockSpec(memory_space=pltpu.VMEM)
    many = len(directions())
    targets = across * along
    slots = sizes[0] * sizes[1] + sizes[2]
    scaled = pl.pallas_call(
        functools.partial(average_kernel, sizes),
        out_shape=jax.ShapeDtypeStruct((across, along, 1, points), jnp.float32),
        in_specs=[pl.BlockSpec(memory_space=pl.ANY)] * 4,
        out_specs=vmem,
        scratch_shapes=[
            pltpu.SMEM((across, 1, along), jnp.int32),
            pltpu.SMEM((across, along, 1, pair_mask.shape[3]), jnp.int32),
            pltpu.VMEM((3, across, along, 1, points), jnp.float32),
            pltpu.VMEM((across, along, 1, points), jnp.float32),
            pltpu.VMEM((2, wide, deep, 4, points), jnp.float32),
            pltpu.VMEM((2, wide, DEPTH, deep * points), jnp.bfloat16),
            pltpu.VMEM((targets, points, DEPTH), jnp.bfloat16),
            pltpu.VMEM((targets, points, points), jnp.float32),
            pltpu.VMEM((targets, points, points), jnp.float32),
            pltpu.VMEM((across, along, points), jnp.float32),
            pltpu.VMEM((slots, 8, points), jnp.float32),
            pltpu.SemaphoreType.DMA((4,)),
            pltpu.SemaphoreType.DMA((many,)),
            pltpu.SemaphoreType.DMA((many,)),
            pltpu.SemaphoreType.DMA((slots,)),
            pltpu.SemaphoreType.DMA((slots,)),
        ],
        compiler_params=pltpu.CompilerParams(collective_id=0, has_side_effects=True, vmem_limit_bytes=FULL_VMEM),
    )(
        counts.transpose(1, 0, 2),
        pair_mask.transpose(1, 2, 0, 3),
        coords.transpose(0, 2, 3, 1, 4),
        strain.transpose(1, 2, 0, 3),
    )
    scaled = scaled.transpose(2, 0, 1, 3)
    kappa_new = jnp.maximum(kappa_old, scaled)
    damage = jnp.where(scaled < 0.0, 0.0, 1.0 - jnp.exp(-(kappa_new - 1.0) / 2.5) / kappa_new)
    return kappa_new, damage


def solution(mesh):
    placed = (
        P(None, "ply", "gx", "gy", None),
        P("ply", "gx", "gy", None),
        P("ply", "gx", "gy", None),
        P("ply", "gx", "gy"),
        P("ply", "gx", "gy", None),
    )
    sizes = tuple(mesh.shape[axis] for axis in AXES)
    return jax.shard_map(
        functools.partial(on_device, sizes),
        mesh=mesh,
        in_specs=placed,
        out_specs=(P("ply", "gx", "gy", None), P("ply", "gx", "gy", None)),
        check_vma=False,
    )
```

```python
import functools

import jax
import jax.numpy as jnp
from jax import lax
from jax.experimental import pallas as pl
from jax.experimental.pallas import tpu as pltpu
from jax.sharding import PartitionSpec as P

MESH = pl.DeviceIdType.MESH
AXES = ("ply", "gx", "gy")
FAR = -1e30
ROWS = 32
DEPTH = 32
AHEAD = 1
FULL_VMEM = 58 * 1024 * 1024


def directions():
    listed = []
    for layer in (0, 1):
        for dx in (-1, 0, 1):
            for dy in (-1, 0, 1):
                if (layer, dx, dy) != (0, 0, 0):
                    listed.append((layer, dx, dy))
    return listed


def send_span(step, size):
    return {-1: (1, 1), 0: (1, size), 1: (size, 1)}[step]


def land_span(step, size):
    return {-1: (0, 1), 0: (1, size), 1: (size + 1, 1)}[step]


def average_kernel(sizes, counts_in, mask_in, coords_in, strain_in, out_ref,
                   counts_ref, mask_ref, coords_ref, strain_ref, pack, source, target_side,
                   total_w, total_s, averaged, held, in_sem, send_sem, recv_sem, max_send, max_recv):
    across, along, _, points = strain_ref.shape
    wide, deep = across + 2, along + 2
    staged = [
        pltpu.make_async_copy(given, kept, in_sem.at[k])
        for k, (given, kept) in enumerate(
            [(counts_in, counts_ref), (coords_in, coords_ref), (strain_in, strain_ref), (mask_in, mask_ref)]
        )
    ]
    for copy in staged:
        copy.start()
    ply, gx, gy = (lax.axis_index(axis) for axis in AXES)
    listed = directions()

    def exists(dx, dy):
        x, y = gx + dx, gy + dy
        return (x >= 0) & (x < sizes[1]) & (y >= 0) & (y < sizes[2])

    def peer(layer, dx, dy):
        return (1 - ply if layer else ply, gx + dx, gy + dy)

    mine = ply * sizes[1] + gx
    first = sizes[0] * sizes[1]
    rounds = (
        [(1 + k, lax.rem(mine + 1 + k, first)) for k in range(first - 1)],
        [(1 + k, lax.rem(gy + 1 + k, sizes[2])) for k in range(sizes[2] - 1)],
    )

    def max_peer(which, index):
        return (index // sizes[1], lax.rem(index, sizes[1]), gy) if which == 0 else (ply, gx, index)

    pack[...] = jnp.zeros(pack.shape, jnp.float32)
    barrier = pltpu.get_barrier_semaphore()
    for layer, dx, dy in listed:
        @pl.when(exists(dx, dy))
        def _():
            pl.semaphore_signal(barrier, inc=1, device_id=peer(layer, dx, dy), device_id_type=MESH)
    for which in range(2):
        for _, index in rounds[which]:
            pl.semaphore_signal(barrier, inc=1, device_id=max_peer(which, index), device_id_type=MESH)

    slots = lax.broadcasted_iota(jnp.int32, (1, points), 1)
    for copy in staged[:3]:
        copy.wait()
    for x in range(across):
        for y in range(along):
            for comp in range(3):
                pack[0, x + 1, y + 1, pl.ds(comp, 1), :] = coords_ref[comp, x, y]
            live = slots < counts_ref[x, 0, y]
            pack[0, x + 1, y + 1, pl.ds(3, 1), :] = jnp.where(live, strain_ref[x, y], 0.0)

    wide_peers = 1 + (gx > 0).astype(jnp.int32) + (gx < sizes[1] - 1).astype(jnp.int32)
    deep_peers = 1 + (gy > 0).astype(jnp.int32) + (gy < sizes[2] - 1).astype(jnp.int32)
    pl.semaphore_wait(barrier, 2 * wide_peers * deep_peers - 1 + len(rounds[0]) + len(rounds[1]))

    def sending(which):
        layer, dx, dy = listed[which]
        (x0, nx), (y0, ny) = send_span(dx, across), send_span(dy, along)
        (u0, _), (v0, _) = land_span(-dx, across), land_span(-dy, along)
        return pltpu.make_async_remote_copy(
            src_ref=pack.at[0, pl.ds(x0, nx), pl.ds(y0, ny)],
            dst_ref=pack.at[layer, pl.ds(u0, nx), pl.ds(v0, ny)],
            send_sem=send_sem.at[which],
            recv_sem=recv_sem.at[which],
            device_id=peer(layer, dx, dy),
            device_id_type=MESH,
        )

    order = sorted(range(len(listed)), key=lambda which: (listed[which][1:] != (0, 0), -listed[which][0]))
    for which in order:
        @pl.when(exists(*listed[which][1:]))
        def _():
            sending(which).start()

    side = (1 - 2 * ply).astype(jnp.float32)
    sub = lax.broadcasted_iota(jnp.int32, (8, points), 0)
    top = sub < 4
    row = jnp.where(top, sub, sub - 4)
    last = jnp.where(top, 1.0, 0.0)

    def split(rows):
        high = rows.astype(jnp.bfloat16).astype(jnp.float32)
        rest = rows - high
        middle = rest.astype(jnp.bfloat16).astype(jnp.float32)
        return high, middle, rest - middle

    def spots(layer, x, y):
        origin = (layer * side - 0.5, x - 0.5 * wide, y - 0.5 * deep)
        found = [
            jnp.broadcast_to(pack[layer, x, y, pl.ds(comp, 1), :], (8, points)) + origin[comp] for comp in range(3)
        ]
        return found, found[0] * found[0] + found[1] * found[1] + found[2] * found[2]

    def stack(rows):
        return jnp.where(row == 0, rows[0], jnp.where(row == 1, rows[1], jnp.where(row == 2, rows[2], rows[3])))

    def build_source(layer, x, y, found, squared):
        strain = jnp.broadcast_to(pack[layer, x, y, pl.ds(3, 1), :], (8, points))
        high, middle, low = split(stack(found + [jnp.where(strain > 0.0, -squared, FAR)]))
        pair = jnp.where(top, high, middle)
        rows = jnp.concatenate([pair, jnp.where(top, high, low), pair, last], 0)
        source[layer, x, :, pl.ds(y * points, points)] = rows.astype(jnp.bfloat16)

    def build_target(x, y, found, squared):
        high, middle, low = split(stack([2.0 * spot for spot in found] + [jnp.ones((8, points), jnp.float32)]))
        a_high, a_middle, a_low = split(1.0 - squared)
        own = jnp.where(sub == 0, a_high, jnp.where(sub == 1, a_middle, jnp.where(sub == 2, a_low, jnp.where(sub == 4, 1.0, 0.0))))
        rows = jnp.concatenate([high, jnp.where(top, middle, high), jnp.where(top, low, middle), own], 0)
        target_side[(x - 1) * along + y - 1] = rows.T.astype(jnp.bfloat16)

    def own_row(x, carry):
        for y in range(1, along + 1):
            found, squared = spots(0, x, y)
            build_source(0, x, y, found, squared)
            build_target(x, y, found, squared)
        return carry

    lax.fori_loop(1, across + 1, own_row, 0, unroll=2)

    staged[3].wait()
    mask_base = jnp.where(ply == 0, 17, 0)

    half_rows = lax.broadcasted_iota(jnp.int32, (DEPTH // 2, points), 0)
    mask_row = jnp.where(half_rows == 12, 1.0, 0.0).astype(jnp.bfloat16)

    def masked_source(layer, x, y, near):
        block = source[layer, x + near // 3, :, pl.ds((y + near % 3) * points, points)]
        if layer == 0 and near == 4:
            return block
        flag = mask_ref[x, y, 0, mask_base + near if layer else 9 + near - (near > 4)]
        away = jnp.full(mask_row.shape, FAR * (1 - flag).astype(jnp.float32)).astype(jnp.bfloat16)
        return jnp.concatenate([block[: DEPTH // 2], block[DEPTH // 2 :] + mask_row * away], 0)

    def row_sums(x, jobs):
        def product(job):
            y, layer = job
            beside = jnp.concatenate([masked_source(layer, x, y, near) for near in range(9)], axis=1)
            return jnp.dot(target_side[x * along + y], beside, preferred_element_type=jnp.float32)

        ready = [product(job) for job in jobs[:AHEAD]]
        for k, (y, layer) in enumerate(jobs):
            if k + AHEAD < len(jobs):
                ready.append(product(jobs[k + AHEAD]))
            inside = ready.pop(0)
            for at in range(0, points, ROWS):
                sum_w = sum_s = None
                for near in range(9):
                    weight = jnp.maximum(inside[at : at + ROWS, near * points : (near + 1) * points], 0.0)
                    weight = weight * weight
                    term = weight * pack[layer, x + near // 3, y + near % 3, pl.ds(3, 1), :]
                    sum_w = weight if near == 0 else sum_w + weight
                    sum_s = term if near == 0 else sum_s + term
                place = (x * along + y, pl.ds(at, ROWS))
                if layer:
                    sum_w = sum_w + total_w[place]
                    sum_s = sum_s + total_s[place]
                total_w[place] = sum_w
                total_s[place] = sum_s

    across_ply = [(y, 1) for y in range(along)]
    whole = [(y, 0) for y in range(along)]

    def inner_row(x, carry):
        row_sums(x, whole[1:-1])
        return carry

    lax.fori_loop(1, across - 1, inner_row, 0, unroll=2)

    for which in order:
        layer, dx, dy = listed[which]

        @pl.when(exists(dx, dy))
        def _():
            (u0, nx), (v0, ny) = land_span(dx, across), land_span(dy, along)
            (x0, _), (y0, _) = send_span(dx, across), send_span(dy, along)
            arriving = pltpu.make_async_remote_copy(
                src_ref=pack.at[0, pl.ds(x0, nx), pl.ds(y0, ny)],
                dst_ref=pack.at[layer, pl.ds(u0, nx), pl.ds(v0, ny)],
                send_sem=send_sem.at[which],
                recv_sem=recv_sem.at[listed.index((layer, -dx, -dy))],
                device_id=peer(layer, dx, dy),
                device_id_type=MESH,
            )
            arriving.wait_recv()
            sending(which).wait_send()

    def halo_row(x, carry):
        for y in range(deep):
            build_source(1, x, y, *spots(1, x, y))
        for y in (0, deep - 1):
            build_source(0, x, y, *spots(0, x, y))
        return carry

    def halo_end(end, carry):
        x = end * (wide - 1)
        for y in range(1, deep - 1):
            build_source(0, x, y, *spots(0, x, y))
        return carry

    lax.fori_loop(0, wide, halo_row, 0, unroll=2)
    lax.fori_loop(0, 2, halo_end, 0, unroll=2)

    def edge_row(x, carry):
        row_sums(x, [whole[0], whole[-1]] + across_ply)
        return carry

    def end_row(end, carry):
        row_sums(end * (across - 1), whole + across_ply)
        return carry

    lax.fori_loop(1, across - 1, edge_row, 0)
    lax.fori_loop(0, 2, end_row, 0)

    ones = jnp.ones((8, 2 * points), jnp.bfloat16)

    def lane_sums(block):
        high = block.astype(jnp.bfloat16)
        low = (block - high.astype(jnp.float32)).astype(jnp.bfloat16)
        both = jnp.concatenate([high, low], axis=1)
        summed = lax.dot_general(ones, both, (((1,), (1,)), ((), ())), preferred_element_type=jnp.float32)
        return summed[0:1]

    def divide(x, carry):
        these = pl.ds(x * along, along)
        weight_sum = lane_sums(total_w[these].reshape(along * points, points))
        weighted = lane_sums(total_s[these].reshape(along * points, points))
        for y in range(along):
            span = slice(y * points, (y + 1) * points)
            live = slots < counts_ref[x, 0, y]
            share = weighted[:, span] / jnp.where(live, weight_sum[:, span], 1.0)
            averaged[x, pl.ds(y, 1), :] = jnp.where(live, share, 0.0)
        return carry

    for x in range(across):
        divide(x, 0)

    best = jnp.max(averaged[...])
    at = 0
    for which in range(2):
        held[at] = jnp.full(held.shape[1:], best, jnp.float32)
        copies = []
        for step, index in rounds[which]:
            copies.append(
                pltpu.make_async_remote_copy(
                    src_ref=held.at[at],
                    dst_ref=held.at[at + step],
                    send_sem=max_send.at[at + step],
                    recv_sem=max_recv.at[at + step],
                    device_id=max_peer(which, index),
                    device_id_type=MESH,
                )
            )
        for copy in copies:
            copy.start()
        for copy in copies:
            copy.wait()
        best = held[at]
        for step, _ in rounds[which]:
            best = jnp.maximum(best, held[at + step])
        best = best if which else jnp.max(best)
        at += len(rounds[which]) + 1

    highest = best[0:1] + 1e-06
    for x in range(across):
        for y in range(along):
            scaled = 4.0 * averaged[x, pl.ds(y, 1), :] / highest
            out_ref[x, y] = jnp.where(slots < counts_ref[x, 0, y], scaled, -1.0)


def on_device(sizes, coords, strain, kappa_old, counts, pair_mask):
    layers, across, along, points = strain.shape
    assert layers == 1 and sizes[0] == 2
    wide, deep = across + 2, along + 2
    vmem = pl.BlockSpec(memory_space=pltpu.VMEM)
    many = len(directions())
    targets = across * along
    slots = sizes[0] * sizes[1] + sizes[2]
    scaled = pl.pallas_call(
        functools.partial(average_kernel, sizes),
        out_shape=jax.ShapeDtypeStruct((across, along, 1, points), jnp.float32),
        in_specs=[pl.BlockSpec(memory_space=pl.ANY)] * 4,
        out_specs=vmem,
        scratch_shapes=[
            pltpu.SMEM((across, 1, along), jnp.int32),
            pltpu.SMEM((across, along, 1, pair_mask.shape[3]), jnp.int32),
            pltpu.VMEM((3, across, along, 1, points), jnp.float32),
            pltpu.VMEM((across, along, 1, points), jnp.float32),
            pltpu.VMEM((2, wide, deep, 4, points), jnp.float32),
            pltpu.VMEM((2, wide, DEPTH, deep * points), jnp.bfloat16),
            pltpu.VMEM((targets, points, DEPTH), jnp.bfloat16),
            pltpu.VMEM((targets, points, points), jnp.float32),
            pltpu.VMEM((targets, points, points), jnp.float32),
            pltpu.VMEM((across, along, points), jnp.float32),
            pltpu.VMEM((slots, 8, points), jnp.float32),
            pltpu.SemaphoreType.DMA((4,)),
            pltpu.SemaphoreType.DMA((many,)),
            pltpu.SemaphoreType.DMA((many,)),
            pltpu.SemaphoreType.DMA((slots,)),
            pltpu.SemaphoreType.DMA((slots,)),
        ],
        compiler_params=pltpu.CompilerParams(collective_id=0, has_side_effects=True, vmem_limit_bytes=FULL_VMEM),
    )(
        counts.transpose(1, 0, 2),
        pair_mask.transpose(1, 2, 0, 3),
        coords.transpose(0, 2, 3, 1, 4),
        strain.transpose(1, 2, 0, 3),
    )
    scaled = scaled.transpose(2, 0, 1, 3)
    kappa_new = jnp.maximum(kappa_old, scaled)
    damage = jnp.where(scaled < 0.0, 0.0, 1.0 - jnp.exp(-(kappa_new - 1.0) / 2.5) / kappa_new)
    return kappa_new, damage


def solution(mesh):
    placed = (
        P(None, "ply", "gx", "gy", None),
        P("ply", "gx", "gy", None),
        P("ply", "gx", "gy", None),
        P("ply", "gx", "gy"),
        P("ply", "gx", "gy", None),
    )
    sizes = tuple(mesh.shape[axis] for axis in AXES)
    return jax.shard_map(
        functools.partial(on_device, sizes),
        mesh=mesh,
        in_specs=placed,
        out_specs=(P("ply", "gx", "gy", None), P("ply", "gx", "gy", None)),
        check_vma=False,
    )
```
